32 devices in a mesh: dp: 4 (over x, core), seq: 4 (over z), tensor: 2 (over y).
Axes of the slice: x: 2, y: 2, z: 4, core: 2. Of those that a mesh axis runs over, the one named last changes fastest.
Arguments:
- memory_in: bfloat16 [8, 588, 1024], P(('dp', 'tensor'), 'seq'), may hold values from -6 to 6
- norm_gain: float32 [1024], replicated, may hold values from 0.1 to 1.9
- qkv_weight: bfloat16 [1024, 1536], replicated, may hold values from -1 to 1
- out_weight: bfloat16 [512, 1024], replicated, may hold values from -0.25 to 0.25
- key_weight: bfloat16 [1024, 1024], replicated, may hold values from -0.1875 to 0.1875
- value_weight: bfloat16 [1024, 1024], replicated, may hold values from -0.1875 to 0.1875
- shift_offsets: int32 [8, 2], P(('dp', 'tensor')), may hold values from 1 to 6
- row_order: int32 [8, 588], P('dp'), may hold values from 0 to 587, each once within a row
Outputs:
- keys: bfloat16 [8, 588, 1024], P('dp', 'tensor', 'seq')
- values: bfloat16 [8, 588, 1024], P('dp', 'tensor', 'seq')
The draws below stay inside these ranges and needn't reach their ends.
All inputs are finite; a program needn't handle non-finite values.
Results may differ from the reference program's by a relative error of at most 0.008.
Values may be sent and summed in bfloat16 or wider, within the bound.
No kernel may reach another device: no remote copies, remote signals or barrier semaphores. Data moves between devices by JAX's collectives and lax.ppermute only.
A program may use at most 64 MiB of HBM per device.

```python
import jax
import jax.numpy as jnp
from jax import lax

EMB = 1024
HEADS = 16
HEAD_DIM = 32
GRID_H = 28
GRID_W = 21
WIN = 7
ROWS = 588
KVW = 1024
PAGES = 8


def draw_memory_in(key, part):
    sample = jnp.clip(jax.random.normal(jax.random.fold_in(key, 23), (PAGES, ROWS, EMB), jnp.float32), -6.0, 6.0)
    return sample.astype(jnp.bfloat16)


def draw_qkv_weight(key, part):
    attn_width = HEADS * HEAD_DIM
    total_width = 3 * attn_width
    sample = jnp.clip(jax.random.normal(jax.random.fold_in(key, 34), (EMB, total_width), jnp.float32), -6.0, 6.0) * EMB ** (-0.5)
    return sample.astype(jnp.bfloat16)


def set_ends(drawn, key, smallest, high):
    shape = drawn.shape
    spot = [jax.random.randint(jax.random.fold_in(key, axis), (), 0, shape[axis]) for axis in range(len(shape))]
    drawn = drawn.at[tuple(spot)].set(smallest)
    longest = shape.index(max(shape))
    spot[longest] = (spot[longest] + 1) % shape[longest]
    return drawn.at[tuple(spot)].set(high)


def scatter_about(key, dims, width, most, held_as=jnp.bfloat16):
    entries = width * jax.random.normal(key, dims, jnp.float32)
    return jnp.clip(entries, min=-most, max=most).astype(held_as)


def setup_inputs(seed: int = 0) -> dict:
    splits = jax.random.split(jax.random.key(seed), 9)
    memory_in = draw_memory_in(jax.random.fold_in(splits[8], 71), 0)
    norm_gain = jnp.clip(1.0 + 0.18 * jax.random.normal(splits[1], (EMB,), jnp.float32), 0.1, 1.9)
    qkv_weight = draw_qkv_weight(jax.random.fold_in(splits[8], 71), 0)
    out_weight = scatter_about(splits[3], (HEADS * HEAD_DIM, EMB), (HEADS * HEAD_DIM) ** -0.5, 0.25)
    key_weight = scatter_about(splits[4], (EMB, KVW), EMB ** -0.5, 0.1875)
    value_weight = scatter_about(splits[5], (EMB, KVW), EMB ** -0.5, 0.1875)
    shift_offsets = set_ends(jax.random.randint(splits[6], (PAGES, 2), 1, WIN), jax.random.fold_in(splits[6], 1), 1, WIN - 1).astype(jnp.int32)
    row_order = jax.vmap(lambda own: jax.random.permutation(own, ROWS))(jax.random.split(splits[7], PAGES)).reshape((PAGES, ROWS)).astype(jnp.int32)
    return dict(memory_in=memory_in, norm_gain=norm_gain, qkv_weight=qkv_weight, out_weight=out_weight, key_weight=key_weight, value_weight=value_weight, shift_offsets=shift_offsets, row_order=row_order)


def window_block(rolled, first_row, row_shift, col_shift, norm_gain, qkv_weight, out_weight):
    row_count = rolled.shape[0] // GRID_W
    attn_width = HEADS * HEAD_DIM
    win_rows = row_count // WIN
    win_cols = GRID_W // WIN
    x_float = rolled.astype(jnp.float32)
    row_mean = lax.optimization_barrier(jnp.mean(x_float, axis=-1, keepdims=True))
    row_var = lax.optimization_barrier(jnp.mean((x_float - row_mean) ** 2, axis=-1, keepdims=True))
    normed = ((x_float - row_mean) * lax.rsqrt(row_var + 1e-05) * norm_gain).astype(jnp.bfloat16)
    projected_qkv = jnp.dot(normed, qkv_weight, preferred_element_type=jnp.float32).astype(jnp.bfloat16)

    def windows(block):
        block = block.reshape(win_rows, WIN, win_cols, WIN, HEADS, HEAD_DIM)
        return block.transpose(0, 2, 4, 1, 3, 5).reshape(win_rows * win_cols, HEADS, WIN * WIN, HEAD_DIM)
    queries = windows(projected_qkv[:, :attn_width]).astype(jnp.float32)
    keys_win = windows(projected_qkv[:, attn_width:2 * attn_width]).astype(jnp.float32)
    values_win = windows(projected_qkv[:, 2 * attn_width:]).astype(jnp.float32)
    scores = jnp.einsum('whqd,whkd->whqk', queries, keys_win) * HEAD_DIM ** (-0.5)
    row_ids = first_row + jnp.arange(row_count, dtype=jnp.int32)
    col_ids = jnp.arange(GRID_W, dtype=jnp.int32)
    wrap_row = (row_ids >= GRID_H - row_shift).astype(jnp.int32)
    wrap_col = (col_ids >= GRID_W - col_shift).astype(jnp.int32)
    labels = 2 * wrap_row[:, None] + wrap_col[None, :]
    labels = labels.reshape(win_rows, WIN, win_cols, WIN).transpose(0, 2, 1, 3).reshape(win_rows * win_cols, WIN * WIN)
    same_region = labels[:, :, None] == labels[:, None, :]
    scores = jnp.where(same_region[:, None], scores, -1000000000.0)
    weights = jax.nn.softmax(scores, axis=-1).astype(jnp.bfloat16)
    attended = jnp.einsum('whqk,whkd->whqd', weights.astype(jnp.float32), values_win).astype(jnp.bfloat16)
    restored = attended.reshape(win_rows, win_cols, HEADS, WIN, WIN, HEAD_DIM)
    restored = restored.transpose(0, 3, 1, 4, 2, 5).reshape(row_count * GRID_W, attn_width)
    return (x_float + jnp.dot(restored, out_weight, preferred_element_type=jnp.float32)).astype(jnp.bfloat16)

def reference(memory_in, norm_gain, qkv_weight, out_weight, key_weight, value_weight, shift_offsets, row_order):

    def per_page(inputs_page):
        page_rows, shifts, row_perm = inputs_page
        page_grid = page_rows.reshape(GRID_H, GRID_W, EMB)
        page_grid = jnp.roll(page_grid, -shifts[0], axis=0)
        page_grid = jnp.roll(page_grid, -shifts[1], axis=1)
        rolled = page_grid.reshape(ROWS, EMB)
        memory = window_block(rolled, 0, shifts[0], shifts[1], norm_gain, qkv_weight, out_weight)
        picked = jnp.take(memory, row_perm, axis=0)
        key_out = jnp.dot(picked, key_weight, preferred_element_type=jnp.float32).astype(jnp.bfloat16)
        value_out = jnp.dot(picked, value_weight, preferred_element_type=jnp.float32).astype(jnp.bfloat16)
        return (key_out, value_out)
    key_rows, value_rows = lax.map(per_page, (memory_in, shift_offsets, row_order))
    return (key_rows, value_rows)
```

```python
import functools

import jax
import jax.numpy as jnp
from jax import lax
from jax.experimental import pallas as pl
from jax.experimental.pallas import tpu as pltpu
from jax.sharding import PartitionSpec as P

HEADS = 16
HEAD_DIM = 32
GRID_H = 28
GRID_W = 21
WIN = 7

GROUP = 8
VMEM_LIMIT = 48 * 1024 * 1024


def rotated(block, axis, distance):
    devices = lax.axis_size(axis)
    return lax.ppermute(block, axis, [(i, (i + distance) % devices) for i in range(devices)])


def dot(a, b):
    return jnp.dot(a, b, preferred_element_type=jnp.float32)


def one_hot(cond):
    return jnp.where(cond, 1.0, 0.0).astype(jnp.bfloat16)


def encode_kernel(
    n_seq, place, shifts, own_ref, halo_ref, gain_ref, qkv_ref, out_ref, key_ref, value_ref, *sent
):
    band_rows = own_ref.shape[0]
    halo_rows = halo_ref.shape[0]
    emb = own_ref.shape[1]
    rows = -(-band_rows // 16) * 16
    attn = HEADS * HEAD_DIM
    seq = place[0]
    row_shift, col_shift = shifts[0, 0], shifts[0, 1]

    cell = lax.broadcasted_iota(jnp.int32, (rows, 1), 0)
    cell_row = cell // GRID_W
    cell_col = cell - cell_row * GRID_W
    from_col = cell_col + col_shift
    from_col = jnp.where(from_col >= GRID_W, from_col - GRID_W, from_col)
    source = jnp.where(cell < band_rows, (cell_row + row_shift) * GRID_W + from_col, -1)
    take_own = one_hot(source == lax.broadcasted_iota(jnp.int32, (rows, band_rows), 1))
    take_halo = one_hot(source - band_rows == lax.broadcasted_iota(jnp.int32, (rows, halo_rows), 1))
    rolled = dot(take_own, own_ref[...]) + dot(take_halo, halo_ref[...])

    mean = jnp.mean(rolled, axis=-1, keepdims=True)
    centred = rolled - mean
    variance = jnp.mean(centred * centred, axis=-1, keepdims=True)
    normed = (centred * lax.rsqrt(variance + 1e-05) * gain_ref[...]).astype(jnp.bfloat16)
    qkv = dot(normed, qkv_ref[...]).astype(jnp.bfloat16)

    def marks(index):
        row = index // GRID_W
        col = index - row * GRID_W
        wrap_row = (seq * WIN + row >= GRID_H - row_shift).astype(jnp.int32)
        wrap_col = (col >= GRID_W - col_shift).astype(jnp.int32)
        return jnp.where(index < band_rows, (col // WIN) * 4 + 2 * wrap_row + wrap_col, -1)

    same = marks(cell) == marks(lax.broadcasted_iota(jnp.int32, (1, rows), 1))
    same = jnp.concatenate([same.astype(jnp.int32)] * GROUP, axis=0) != 0

    width = GROUP * HEAD_DIM
    lane_head = lax.broadcasted_iota(jnp.int32, (1, width), 1) // HEAD_DIM
    parts = []
    for g in range(HEADS // GROUP):
        at = g * width
        q = qkv[:, at : at + width]
        k = qkv[:, attn + at : attn + at + width]
        v = qkv[:, 2 * attn + at : 2 * attn + at + width]
        stacked = jnp.concatenate(
            [jnp.where(lane_head == h, q, jnp.zeros_like(q)) for h in range(GROUP)], axis=0
        )
        scores = lax.dot_general(
            stacked, k, (((1,), (1,)), ((), ())), preferred_element_type=jnp.float32
        )
        scores = jnp.where(same, scores * HEAD_DIM ** (-0.5), -1000000000.0)
        scores = jnp.exp(scores - jnp.max(scores, axis=-1, keepdims=True))
        total = jnp.sum(scores, axis=-1, keepdims=True)
        weights = (scores * (1.0 / total)).astype(jnp.bfloat16)
        mixed = dot(weights, v)
        part = jnp.zeros((rows, width), jnp.float32)
        for h in range(GROUP):
            part = jnp.where(lane_head == h, mixed[h * rows : (h + 1) * rows], part)
        parts.append(part.astype(jnp.bfloat16))
    attended = jnp.concatenate(parts, axis=1)
    memory = (rolled + dot(attended, out_ref[...])).astype(jnp.bfloat16)

    own_cols = key_ref.shape[1] // n_seq
    for d in range(n_seq):
        to = lax.rem(seq + d, n_seq)
        cols = pl.ds(pl.multiple_of(to * own_cols, own_cols), own_cols)
        sent[d][:, :own_cols] = dot(memory, key_ref[:, cols])[:band_rows].astype(jnp.bfloat16)
        sent[d][:, own_cols:] = dot(memory, value_ref[:, cols])[:band_rows].astype(jnp.bfloat16)


def select_kernel(n_seq, first, count, place, order_ref, *refs):
    held, outs = refs[:n_seq], refs[n_seq:]
    band_rows = held[0].shape[0]
    seq, tensor = place[0], place[1]
    n_tensor = order_ref.shape[0]
    pos = order_ref.shape[1]
    for i in range(count):
        order = order_ref[lax.rem(tensor + first + i, n_tensor)]
        total = None
        for d in range(n_seq):
            band = lax.rem(seq - d + n_seq, n_seq)
            pick = one_hot(
                order - band * band_rows == lax.broadcasted_iota(jnp.int32, (pos, band_rows), 1)
            )
            term = dot(pick, held[d][...])
            total = term if total is None else total + term
        outs[i][...] = total.astype(jnp.bfloat16)


def join_kernel(place, *refs):
    blocks, (key_out, value_out) = refs[:-2], refs[-2:]
    n_tensor = len(blocks)
    own_cols = key_out.shape[-1]
    for d in range(n_tensor):
        page = lax.rem(place[1] - d + n_tensor, n_tensor)
        key_out[page] = blocks[d][:, :own_cols]
        value_out[page] = blocks[d][:, own_cols:]


def call(kernel, out_shape, n_scalar, n_vmem, flops, moved):
    smem = pl.BlockSpec(memory_space=pltpu.SMEM)
    vmem = pl.BlockSpec(memory_space=pltpu.VMEM)
    return pl.pallas_call(
        kernel,
        out_shape=out_shape,
        in_specs=[smem] * n_scalar + [vmem] * n_vmem,
        out_specs=jax.tree.map(lambda _: vmem, out_shape),
        compiler_params=pltpu.CompilerParams(vmem_limit_bytes=VMEM_LIMIT),
        cost_estimate=pl.CostEstimate(flops=flops, bytes_accessed=moved, transcendentals=0),
    )


def local(
    memory_in, norm_gain, qkv_weight, out_weight, key_weight, value_weight, shift_offsets, row_order
):
    _, band_rows, emb = memory_in.shape
    n_seq = lax.axis_size("seq")
    n_tensor = lax.axis_size("tensor")
    own_cols = key_weight.shape[1] // n_seq
    pos = row_order.shape[1] // n_tensor
    place = jnp.stack([lax.axis_index("seq"), lax.axis_index("tensor")]).astype(jnp.int32)
    own = memory_in[0]
    halo = rotated(own[: (WIN - 1) * GRID_W], "seq", -1)
    order = lax.dynamic_index_in_dim(row_order, lax.axis_index("tensor"), 0, False)
    order = order.reshape(n_tensor, pos, 1)

    block = jax.ShapeDtypeStruct((band_rows, 2 * own_cols), jnp.bfloat16)
    sent = call(
        functools.partial(encode_kernel, n_seq), [block] * n_seq, 2, 7, 2_500_000_000, 10_000_000
    )(
        place, shift_offsets, own, halo, norm_gain.reshape(1, emb), qkv_weight, out_weight,
        key_weight, value_weight,
    )
    held = [rotated(sent[d], "seq", d) if d else sent[0] for d in range(n_seq)]

    piece = jax.ShapeDtypeStruct((pos, 2 * own_cols), jnp.bfloat16)
    away = call(
        functools.partial(select_kernel, n_seq, 1, n_tensor - 1),
        [piece] * (n_tensor - 1), 1, 1 + n_seq, 600_000_000, 1_000_000,
    )(place, order, *held)
    arrived = [rotated(away[d - 1], "tensor", d) for d in range(1, n_tensor)]
    kept = call(
        functools.partial(select_kernel, n_seq, 0, 1),
        [piece], 1, 1 + n_seq, 600_000_000, 1_000_000,
    )(place, order, *held)
    out = jax.ShapeDtypeStruct((n_tensor, pos, own_cols), jnp.bfloat16)
    key_out, value_out = call(join_kernel, [out, out], 1, n_tensor, 0, 2_000_000)(
        place, kept[0], *arrived
    )
    return key_out, value_out


def solution(mesh):
    placed = (
        P(("dp", "tensor"), "seq", None),
        P(),
        P(),
        P(),
        P(),
        P(),
        P(("dp", "tensor"), None),
        P("dp", None),
    )
    return jax.shard_map(
        local,
        mesh=mesh,
        in_specs=placed,
        out_specs=(P("dp", "tensor", "seq"), P("dp", "tensor", "seq")),
        check_vma=False,
    )
```

```python
import functools

import jax
import jax.numpy as jnp
from jax import lax
from jax.experimental import pallas as pl
from jax.experimental.pallas import tpu as pltpu
from jax.sharding import PartitionSpec as P

HEADS = 16
HEAD_DIM = 32
GRID_H = 28
GRID_W = 21
WIN = 7

GROUP = 8
VMEM_LIMIT = 32 * 1024 * 1024


def rotated(block, axis, distance):
    devices = lax.axis_size(axis)
    return lax.ppermute(block, axis, [(i, (i + distance) % devices) for i in range(devices)])


def dot(a, b):
    return jnp.dot(a, b, preferred_element_type=jnp.float32)


def one_hot(cond):
    return jnp.where(cond, 1.0, 0.0).astype(jnp.bfloat16)


def stage_kernel(n_weights, shifts, pages_ref, *refs):
    weights, rolled_ref, staged = refs[:n_weights], refs[n_weights], refs[n_weights + 1 : -2]
    own, arrived = refs[-2:]
    copies = [pltpu.make_async_copy(pages_ref.at[0], own, arrived.at[n_weights])]
    copies += [
        pltpu.make_async_copy(weights[i], staged[i], arrived.at[i]) for i in range(n_weights)
    ]
    for copy in copies:
        copy.start()
    band_rows = own.shape[0]
    rows = rolled_ref.shape[0]
    source = roll_source(rows, band_rows, shifts)
    take = one_hot(source == lax.broadcasted_iota(jnp.int32, (rows, band_rows), 1))
    copies[0].wait()
    rolled_ref[...] = dot(take, own[...]).astype(jnp.bfloat16)
    for copy in copies[1:]:
        copy.wait()


def roll_source(rows, band_rows, shifts):
    cell = lax.broadcasted_iota(jnp.int32, (rows, 1), 0)
    cell_row = cell // GRID_W
    from_col = cell - cell_row * GRID_W + shifts[0, 1]
    from_col = jnp.where(from_col >= GRID_W, from_col - GRID_W, from_col)
    return jnp.where(cell < band_rows, (cell_row + shifts[0, 0]) * GRID_W + from_col, -1)


def encode_kernel(
    n_seq, band_rows, place, shifts, rolled_ref, halo_ref, gain_ref, qkv_ref, out_ref, key_ref,
    memory_ref, *sent
):
    halo_rows = halo_ref.shape[0]
    rows = rolled_ref.shape[0]
    attn = HEADS * HEAD_DIM
    seq = place[0]
    row_shift, col_shift = shifts[0, 0], shifts[0, 1]

    source = roll_source(rows, band_rows, shifts) - band_rows
    take = one_hot(source == lax.broadcasted_iota(jnp.int32, (rows, halo_rows), 1))
    rolled = rolled_ref[...].astype(jnp.float32) + dot(take, halo_ref[...])

    mean = jnp.mean(rolled, axis=-1, keepdims=True)
    centred = rolled - mean
    variance = jnp.mean(centred * centred, axis=-1, keepdims=True)
    normed = (centred * lax.rsqrt(variance + 1e-05) * gain_ref[...]).astype(jnp.bfloat16)
    qkv = dot(normed, qkv_ref[...]).astype(jnp.bfloat16)

    def marks(index):
        row = index // GRID_W
        col = index - row * GRID_W
        wrap_row = (seq * WIN + row >= GRID_H - row_shift).astype(jnp.int32)
        wrap_col = (col >= GRID_W - col_shift).astype(jnp.int32)
        return jnp.where(index < band_rows, (col // WIN) * 4 + 2 * wrap_row + wrap_col, -1)

    same = marks(lax.broadcasted_iota(jnp.int32, (rows, 1), 0)) == marks(
        lax.broadcasted_iota(jnp.int32, (1, rows), 1)
    )
    same = jnp.concatenate([same.astype(jnp.int32)] * GROUP, axis=0) != 0

    width = GROUP * HEAD_DIM
    lane_head = lax.broadcasted_iota(jnp.int32, (1, width), 1) // HEAD_DIM
    parts = []
    for g in range(HEADS // GROUP):
        at = g * width
        q = qkv[:, at : at + width]
        k = qkv[:, attn + at : attn + at + width]
        v = qkv[:, 2 * attn + at : 2 * attn + at + width]
        stacked = jnp.concatenate(
            [jnp.where(lane_head == h, q, jnp.zeros_like(q)) for h in range(GROUP)], axis=0
        )
        scores = lax.dot_general(
            stacked, k, (((1,), (1,)), ((), ())), preferred_element_type=jnp.float32
        )
        scores = jnp.where(same, scores * HEAD_DIM ** (-0.5), -1000000000.0)
        scores = jnp.exp(scores - jnp.max(scores, axis=-1, keepdims=True))
        total = jnp.sum(scores, axis=-1, keepdims=True)
        weights = (scores * (1.0 / total)).astype(jnp.bfloat16)
        mixed = dot(weights, v)
        part = jnp.zeros((rows, width), jnp.float32)
        for h in range(GROUP):
            part = jnp.where(lane_head == h, mixed[h * rows : (h + 1) * rows], part)
        parts.append(part.astype(jnp.bfloat16))
    attended = jnp.concatenate(parts, axis=1)
    memory = (rolled + dot(attended, out_ref[...])).astype(jnp.bfloat16)
    memory_ref[...] = memory
    project(n_seq, seq, memory, key_ref, sent)


def project(n_seq, seq, memory, weight_ref, sent):
    own_cols = weight_ref.shape[1] // n_seq
    for d in range(n_seq):
        to = lax.rem(seq + d, n_seq)
        cols = pl.ds(pl.multiple_of(to * own_cols, own_cols), own_cols)
        block = dot(memory, weight_ref[:, cols])
        sent[d][...] = block[: sent[d].shape[0]].astype(jnp.bfloat16)


def value_kernel(n_seq, place, memory_ref, weight_ref, *sent):
    project(n_seq, place[0], memory_ref[...], weight_ref, sent)


def select_kernel(n_seq, first, count, place, order_ref, *refs):
    held, outs = refs[:n_seq], refs[n_seq:]
    band_rows = held[0].shape[0]
    seq, tensor = place[0], place[1]
    n_tensor = order_ref.shape[0]
    pos = order_ref.shape[1]
    for i in range(count):
        order = order_ref[lax.rem(tensor + first + i, n_tensor)]
        total = None
        for d in range(n_seq):
            band = lax.rem(seq - d + n_seq, n_seq)
            pick = one_hot(
                order - band * band_rows == lax.broadcasted_iota(jnp.int32, (pos, band_rows), 1)
            )
            term = dot(pick, held[d][...])
            total = term if total is None else total + term
        outs[i][...] = total.astype(jnp.bfloat16)


def call(kernel, out_shape, n_scalar, n_vmem, flops, moved, n_hbm=0, scratch=()):
    smem = pl.BlockSpec(memory_space=pltpu.SMEM)
    vmem = pl.BlockSpec(memory_space=pltpu.VMEM)
    hbm = pl.BlockSpec(memory_space=pltpu.HBM)
    return pl.pallas_call(
        kernel,
        out_shape=out_shape,
        in_specs=[smem] * n_scalar + [vmem] * n_vmem + [hbm] * n_hbm,
        out_specs=jax.tree.map(lambda _: vmem, out_shape),
        scratch_shapes=list(scratch),
        compiler_params=pltpu.CompilerParams(vmem_limit_bytes=VMEM_LIMIT),
        cost_estimate=pl.CostEstimate(flops=flops, bytes_accessed=moved, transcendentals=0),
    )


def local(
    memory_in, norm_gain, qkv_weight, out_weight, key_weight, value_weight, shift_offsets, row_order
):
    _, band_rows, emb = memory_in.shape
    n_seq = lax.axis_size("seq")
    n_tensor = lax.axis_size("tensor")
    own_cols = key_weight.shape[1] // n_seq
    pos = row_order.shape[1] // n_tensor
    rows = -(-band_rows // 16) * 16
    place = jnp.stack([lax.axis_index("seq"), lax.axis_index("tensor")]).astype(jnp.int32)
    halo = rotated(memory_in[0, : (WIN - 1) * GRID_W], "seq", -1)
    order = lax.dynamic_index_in_dim(row_order, lax.axis_index("tensor"), 0, False)
    order = order.reshape(n_tensor, pos, 1)

    weights = [qkv_weight, out_weight, key_weight, value_weight]
    rolled_own, *weights = call(
        functools.partial(stage_kernel, len(weights)),
        [jax.ShapeDtypeStruct((rows, emb), jnp.bfloat16)]
        + [jax.ShapeDtypeStruct(w.shape, w.dtype) for w in weights],
        1, 0, 50_000_000, 16_000_000, 1 + len(weights),
        [
            pltpu.VMEM((band_rows, emb), jnp.bfloat16),
            pltpu.SemaphoreType.DMA((1 + len(weights),)),
        ],
    )(shift_offsets, memory_in, *weights)

    block = jax.ShapeDtypeStruct((band_rows, own_cols), jnp.bfloat16)
    memory, *key_sent = call(
        functools.partial(encode_kernel, n_seq, band_rows),
        [jax.ShapeDtypeStruct((rows, emb), jnp.bfloat16)] + [block] * n_seq,
        2, 6, 1_600_000_000, 8_000_000,
    )(place, shift_offsets, rolled_own, halo, norm_gain.reshape(1, emb), *weights[:3])
    value_sent = call(
        functools.partial(value_kernel, n_seq), [block] * n_seq, 1, 2, 300_000_000, 2_000_000
    )(place, memory, weights[3])

    piece = jax.ShapeDtypeStruct((pos, own_cols), jnp.bfloat16)

    def gathered(sent):
        held = [rotated(sent[d], "seq", d) if d else sent[0] for d in range(n_seq)]
        away = call(
            functools.partial(select_kernel, n_seq, 1, n_tensor - 1),
            [piece] * (n_tensor - 1), 1, 1 + n_seq, 300_000_000, 1_000_000,
        )(place, order, *held)
        arrived = [rotated(away[d - 1], "tensor", d) for d in range(1, n_tensor)]
        kept = call(
            functools.partial(select_kernel, n_seq, 0, 1),
            [piece], 1, 1 + n_seq, 300_000_000, 1_000_000,
        )(place, order, *held)
        page = jnp.arange(n_tensor)[:, None, None]
        result = kept[0][None]
        for d in range(1, n_tensor):
            came = page == (lax.axis_index("tensor") - d) % n_tensor
            result = jnp.where(came, arrived[d - 1][None], result)
        return jnp.broadcast_to(result, (n_tensor, pos, own_cols))

    return gathered(key_sent), gathered(value_sent)


def solution(mesh):
    placed = (
        P(("dp", "tensor"), "seq", None),
        P(),
        P(),
        P(),
        P(),
        P(),
        P(("dp", "tensor"), None),
        P("dp", None),
    )
    return jax.shard_map(
        local,
        mesh=mesh,
        in_specs=placed,
        out_specs=(P("dp", "tensor", "seq"), P("dp", "tensor", "seq")),
        check_vma=False,
    )
```

```python
import functools

import jax
import jax.numpy as jnp
from jax import lax
from jax.experimental import pallas as pl
from jax.experimental.pallas import tpu as pltpu
from jax.sharding import PartitionSpec as P

HEADS = 16
HEAD_DIM = 32
GRID_H = 28
GRID_W = 21
WIN = 7

GROUP = 8
VMEM_LIMIT = 32 * 1024 * 1024
ENCODE_LIMIT = 52 * 1024 * 1024


def rotated(block, axis, distance):
    devices = lax.axis_size(axis)
    return lax.ppermute(block, axis, [(i, (i + distance) % devices) for i in range(devices)])


def dot(a, b):
    return jnp.dot(a, b, preferred_element_type=jnp.float32)


def one_hot(cond):
    return jnp.where(cond, 1.0, 0.0).astype(jnp.bfloat16)


def stage_kernel(place, pages_ref, gain_ref, rolled_ref, gain_out):
    gain_out[...] = gain_ref[...]
    band_rows = pages_ref.shape[1]
    rows = rolled_ref.shape[0]
    source = roll_source(rows, band_rows, place)
    take = one_hot(source == lax.broadcasted_iota(jnp.int32, (rows, band_rows), 1))
    rolled_ref[...] = dot(take, pages_ref[0]).astype(jnp.bfloat16)


def roll_source(rows, band_rows, place):
    cell = lax.broadcasted_iota(jnp.int32, (rows, 1), 0)
    cell_row = cell // GRID_W
    from_col = cell - cell_row * GRID_W + place[3]
    from_col = jnp.where(from_col >= GRID_W, from_col - GRID_W, from_col)
    return jnp.where(cell < band_rows, (cell_row + place[2]) * GRID_W + from_col, -1)


def encode_kernel(
    n_seq, band_rows, place, rolled_ref, halo_ref, gain_ref, qkv_hbm, out_hbm, key_hbm,
    memory_ref, *refs
):
    sent, (qkv_ref, out_ref, key_ref, arrived) = refs[:n_seq], refs[n_seq:]
    halo_rows = halo_ref.shape[0]
    rows = rolled_ref.shape[0]
    attn = HEADS * HEAD_DIM
    seq = place[0]
    thirds = [pl.ds(i * attn, attn) for i in range(3)]
    pairs = [(qkv_hbm.at[:, third], qkv_ref.at[:, third]) for third in thirds]
    pairs += [(out_hbm, out_ref), (key_hbm, key_ref)]
    copies = [pltpu.make_async_copy(*pair, arrived.at[i]) for i, pair in enumerate(pairs)]
    for copy in copies:
        copy.start()
    row_shift, col_shift = place[2], place[3]

    source = roll_source(rows, band_rows, place) - band_rows
    take = one_hot(source == lax.broadcasted_iota(jnp.int32, (rows, halo_rows), 1))
    rolled = rolled_ref[...].astype(jnp.float32) + dot(take, halo_ref[...])

    mean = jnp.mean(rolled, axis=-1, keepdims=True)
    centred = rolled - mean
    variance = jnp.mean(centred * centred, axis=-1, keepdims=True)
    normed = (centred * lax.rsqrt(variance + 1e-05) * gain_ref[...]).astype(jnp.bfloat16)
    parts = []
    for third, copy in zip(thirds, copies):
        copy.wait()
        parts.append(dot(normed, qkv_ref[:, third]).astype(jnp.bfloat16))
    queries, keys, values = parts

    def marks(index):
        row = index // GRID_W
        col = index - row * GRID_W
        wrap_row = (seq * WIN + row >= GRID_H - row_shift).astype(jnp.int32)
        wrap_col = (col >= GRID_W - col_shift).astype(jnp.int32)
        return jnp.where(index < band_rows, (col // WIN) * 4 + 2 * wrap_row + wrap_col, -1)

    same = marks(lax.broadcasted_iota(jnp.int32, (rows, 1), 0)) == marks(
        lax.broadcasted_iota(jnp.int32, (1, rows), 1)
    )
    same = jnp.concatenate([same.astype(jnp.int32)] * GROUP, axis=0) != 0

    width = GROUP * HEAD_DIM
    lane_head = lax.broadcasted_iota(jnp.int32, (1, width), 1) // HEAD_DIM
    parts = []
    for g in range(HEADS // GROUP):
        at = g * width
        q, k, v = (part[:, at : at + width] for part in (queries, keys, values))
        stacked = jnp.concatenate(
            [jnp.where(lane_head == h, q, jnp.zeros_like(q)) for h in range(GROUP)], axis=0
        )
        scores = lax.dot_general(
            stacked, k, (((1,), (1,)), ((), ())), preferred_element_type=jnp.float32
        )
        scores = jnp.where(same, scores * HEAD_DIM ** (-0.5), -1000000000.0)
        scores = jnp.exp(scores - jnp.max(scores, axis=-1, keepdims=True))
        total = jnp.sum(scores, axis=-1, keepdims=True)
        weights = (scores * (1.0 / total)).astype(jnp.bfloat16)
        mixed = dot(weights, v)
        part = jnp.zeros((rows, width), jnp.float32)
        for h in range(GROUP):
            part = jnp.where(lane_head == h, mixed[h * rows : (h + 1) * rows], part)
        parts.append(part.astype(jnp.bfloat16))
    attended = jnp.concatenate(parts, axis=1)
    copies[3].wait()
    memory = (rolled + dot(attended, out_ref[...])).astype(jnp.bfloat16)
    memory_ref[...] = memory
    copies[4].wait()
    project(n_seq, seq, memory, key_ref, sent)


def project(n_seq, seq, memory, weight_ref, sent):
    own_cols = weight_ref.shape[1] // n_seq
    for d in range(n_seq):
        to = lax.rem(seq + d, n_seq)
        cols = pl.ds(pl.multiple_of(to * own_cols, own_cols), own_cols)
        block = dot(memory, weight_ref[:, cols])
        sent[d][...] = block[: sent[d].shape[0]].astype(jnp.bfloat16)


def value_kernel(n_seq, place, memory_ref, weight_ref, *sent):
    project(n_seq, place[0], memory_ref[...], weight_ref, sent)


def select_kernel(n_seq, first, count, place, order_ref, *refs):
    held, outs = refs[:n_seq], refs[n_seq:]
    band_rows = held[0].shape[0]
    seq, tensor = place[0], place[1]
    n_tensor = order_ref.shape[0]
    pos = order_ref.shape[1]
    for i in range(count):
        order = order_ref[lax.rem(tensor + first + i, n_tensor)]
        total = None
        for d in range(n_seq):
            band = lax.rem(seq - d + n_seq, n_seq)
            pick = one_hot(
                order - band * band_rows == lax.broadcasted_iota(jnp.int32, (pos, band_rows), 1)
            )
            term = dot(pick, held[d][...])
            total = term if total is None else total + term
        outs[i][...] = total.astype(jnp.bfloat16)


def call(kernel, out_shape, n_scalar, n_vmem, flops, moved, n_hbm=0, scratch=(), limit=VMEM_LIMIT):
    smem = pl.BlockSpec(memory_space=pltpu.SMEM)
    vmem = pl.BlockSpec(memory_space=pltpu.VMEM)
    hbm = pl.BlockSpec(memory_space=pltpu.HBM)
    return pl.pallas_call(
        kernel,
        out_shape=out_shape,
        in_specs=[smem] * n_scalar + [vmem] * n_vmem + [hbm] * n_hbm,
        out_specs=jax.tree.map(lambda _: vmem, out_shape),
        scratch_shapes=list(scratch),
        compiler_params=pltpu.CompilerParams(vmem_limit_bytes=limit),
        cost_estimate=pl.CostEstimate(flops=flops, bytes_accessed=moved, transcendentals=0),
    )


def local(
    memory_in, norm_gain, qkv_weight, out_weight, key_weight, value_weight, shift_offsets, row_order
):
    _, band_rows, emb = memory_in.shape
    n_seq = lax.axis_size("seq")
    n_tensor = lax.axis_size("tensor")
    own_cols = key_weight.shape[1] // n_seq
    pos = row_order.shape[1] // n_tensor
    rows = -(-band_rows // 16) * 16
    place = jnp.stack(
        [lax.axis_index("seq"), lax.axis_index("tensor"), shift_offsets[0, 0], shift_offsets[0, 1]]
    )
    halo = rotated(memory_in[0, : (WIN - 1) * GRID_W], "seq", -1)
    order = lax.dynamic_index_in_dim(row_order, lax.axis_index("tensor"), 0, False)
    order = order.reshape(n_tensor, pos, 1)

    rolled_own, gain = call(
        stage_kernel,
        [
            jax.ShapeDtypeStruct((rows, emb), jnp.bfloat16),
            jax.ShapeDtypeStruct((1, emb), jnp.float32),
        ],
        1, 2, 50_000_000, 1_000_000,
    )(place, memory_in, norm_gain.reshape(1, emb))
    weights = [qkv_weight, out_weight, key_weight]
    block = jax.ShapeDtypeStruct((band_rows, own_cols), jnp.bfloat16)
    memory, *key_sent = call(
        functools.partial(encode_kernel, n_seq, band_rows),
        [jax.ShapeDtypeStruct((rows, emb), jnp.bfloat16)] + [block] * n_seq,
        1, 3, 1_600_000_000, 8_000_000, len(weights),
        [pltpu.VMEM(w.shape, w.dtype) for w in weights] + [pltpu.SemaphoreType.DMA((5,))],
        ENCODE_LIMIT,
    )(place, rolled_own, halo, gain, *weights)
    value_sent = call(
        functools.partial(value_kernel, n_seq), [block] * n_seq, 1, 2, 300_000_000, 2_000_000
    )(place, memory, value_weight)

    piece = jax.ShapeDtypeStruct((pos, own_cols), jnp.bfloat16)

    def gathered(sent):
        held = [rotated(sent[d], "seq", d) if d else sent[0] for d in range(n_seq)]
        away = call(
            functools.partial(select_kernel, n_seq, 1, n_tensor - 1),
            [piece] * (n_tensor - 1), 1, 1 + n_seq, 300_000_000, 1_000_000,
        )(place, order, *held)
        arrived = [rotated(away[d - 1], "tensor", d) for d in range(1, n_tensor)]
        kept = call(
            functools.partial(select_kernel, n_seq, 0, 1),
            [piece], 1, 1 + n_seq, 300_000_000, 1_000_000,
        )(place, order, *held)
        return [*kept, *arrived]

    def by_page(blocks):
        page = jnp.arange(n_tensor)[:, None, None]
        result = blocks[0][None]
        for d in range(1, n_tensor):
            came = page == (lax.axis_index("tensor") - d) % n_tensor
            result = jnp.where(came, blocks[d][None], result)
        return jnp.broadcast_to(result, (n_tensor, pos, own_cols))

    key_out, value_blocks = lax.optimization_barrier((by_page(gathered(key_sent)), gathered(value_sent)))
    return key_out, by_page(value_blocks)


def solution(mesh):
    placed = (
        P(("dp", "tensor"), "seq", None),
        P(),
        P(),
        P(),
        P(),
        P(),
        P(("dp", "tensor"), None),
        P("dp", None),
    )
    return jax.shard_map(
        local,
        mesh=mesh,
        in_specs=placed,
        out_specs=(P("dp", "tensor", "seq"), P("dp", "tensor", "seq")),
        check_vma=False,
    )
```

```python
import functools

import jax
import jax.numpy as jnp
from jax import lax
from jax.experimental import pallas as pl
from jax.experimental.pallas import tpu as pltpu
from jax.sharding import PartitionSpec as P

HEADS = 16
HEAD_DIM = 32
GRID_H = 28
GRID_W = 21
WIN = 7

GROUP = 8
VMEM_LIMIT = 32 * 1024 * 1024
STAGE_LIMIT = 48 * 1024 * 1024
ENCODE_LIMIT = 52 * 1024 * 1024

SMEM = pl.BlockSpec(memory_space=pltpu.SMEM)
VMEM = pl.BlockSpec(memory_space=pltpu.VMEM)
HBM = pl.BlockSpec(memory_space=pltpu.HBM)


def rotated(block, axis, distance):
    devices = lax.axis_size(axis)
    return lax.ppermute(block, axis, [(i, (i + distance) % devices) for i in range(devices)])


def dot(a, b):
    return jnp.dot(a, b, preferred_element_type=jnp.float32)


def one_hot(cond):
    return jnp.where(cond, 1.0, 0.0).astype(jnp.bfloat16)


def stage_kernel(shifts, pages_ref, gain_ref, weight_hbm, rolled_ref, gain_out, weight_ref, arrived):
    copy = pltpu.make_async_copy(weight_hbm, weight_ref, arrived)
    copy.start()
    gain_out[...] = gain_ref[...]
    band_rows = pages_ref.shape[1]
    rows = rolled_ref.shape[0]
    source = roll_source(rows, band_rows, shifts)
    take = one_hot(source == lax.broadcasted_iota(jnp.int32, (rows, band_rows), 1))
    rolled_ref[...] = dot(take, pages_ref[0]).astype(jnp.bfloat16)
    copy.wait()


def roll_source(rows, band_rows, shifts):
    cell = lax.broadcasted_iota(jnp.int32, (rows, 1), 0)
    cell_row = cell // GRID_W
    from_col = cell - cell_row * GRID_W + shifts[0, 1]
    from_col = jnp.where(from_col >= GRID_W, from_col - GRID_W, from_col)
    return jnp.where(cell < band_rows, (cell_row + shifts[0, 0]) * GRID_W + from_col, -1)


def encode_kernel(
    n_seq, band_rows, place, shifts, rolled_ref, halo_ref, gain_ref, qkv_ref, *refs
):
    in_hbm, refs = refs[:3], refs[3:]
    key_sent, value_sent, refs = refs[:n_seq], refs[n_seq : 2 * n_seq], refs[2 * n_seq :]
    on_chip, arrived = refs[:3], refs[3]
    out_ref, key_ref, value_ref = on_chip
    copies = [
        pltpu.make_async_copy(in_hbm[i], on_chip[i], arrived.at[i]) for i in range(len(on_chip))
    ]
    for copy in copies:
        copy.start()
    halo_rows = halo_ref.shape[0]
    rows = rolled_ref.shape[0]
    attn = HEADS * HEAD_DIM
    seq = place[0]
    row_shift, col_shift = shifts[0, 0], shifts[0, 1]

    source = roll_source(rows, band_rows, shifts) - band_rows
    take = one_hot(source == lax.broadcasted_iota(jnp.int32, (rows, halo_rows), 1))
    rolled = rolled_ref[...].astype(jnp.float32) + dot(take, halo_ref[...])

    mean = jnp.mean(rolled, axis=-1, keepdims=True)
    centred = rolled - mean
    variance = jnp.mean(centred * centred, axis=-1, keepdims=True)
    normed = (centred * lax.rsqrt(variance + 1e-05) * gain_ref[...]).astype(jnp.bfloat16)
    qkv = dot(normed, qkv_ref[...]).astype(jnp.bfloat16)
    queries, keys, values = (qkv[:, i * attn : (i + 1) * attn] for i in range(3))

    def marks(index):
        row = index // GRID_W
        col = index - row * GRID_W
        wrap_row = (seq * WIN + row >= GRID_H - row_shift).astype(jnp.int32)
        wrap_col = (col >= GRID_W - col_shift).astype(jnp.int32)
        return jnp.where(index < band_rows, (col // WIN) * 4 + 2 * wrap_row + wrap_col, -1)

    same = marks(lax.broadcasted_iota(jnp.int32, (rows, 1), 0)) == marks(
        lax.broadcasted_iota(jnp.int32, (1, rows), 1)
    )
    same = jnp.concatenate([same.astype(jnp.int32)] * GROUP, axis=0) != 0

    width = GROUP * HEAD_DIM
    lane_head = lax.broadcasted_iota(jnp.int32, (1, width), 1) // HEAD_DIM
    parts = []
    for g in range(HEADS // GROUP):
        at = g * width
        q, k, v = (part[:, at : at + width] for part in (queries, keys, values))
        stacked = jnp.concatenate(
            [jnp.where(lane_head == h, q, jnp.zeros_like(q)) for h in range(GROUP)], axis=0
        )
        scores = lax.dot_general(
            stacked, k, (((1,), (1,)), ((), ())), preferred_element_type=jnp.float32
        )
        scores = jnp.where(same, scores * HEAD_DIM ** (-0.5), -1000000000.0)
        scores = jnp.exp(scores - jnp.max(scores, axis=-1, keepdims=True))
        total = jnp.sum(scores, axis=-1, keepdims=True)
        weights = (scores * (1.0 / total)).astype(jnp.bfloat16)
        mixed = dot(weights, v)
        part = jnp.zeros((rows, width), jnp.float32)
        for h in range(GROUP):
            part = jnp.where(lane_head == h, mixed[h * rows : (h + 1) * rows], part)
        parts.append(part.astype(jnp.bfloat16))
    attended = jnp.concatenate(parts, axis=1)
    copies[0].wait()
    memory = (rolled + dot(attended, out_ref[...])).astype(jnp.bfloat16)
    copies[1].wait()
    project(n_seq, seq, memory, key_ref, key_sent)
    copies[2].wait()
    project(n_seq, seq, memory, value_ref, value_sent)


def project(n_seq, seq, memory, weight_ref, sent):
    own_cols = weight_ref.shape[1] // n_seq
    for d in range(n_seq):
        to = lax.rem(seq + d, n_seq)
        cols = pl.ds(pl.multiple_of(to * own_cols, own_cols), own_cols)
        block = dot(memory, weight_ref[:, cols])
        sent[d][...] = block[: sent[d].shape[0]].astype(jnp.bfloat16)


def select_kernel(n_seq, first, count, place, order_ref, *refs):
    held, outs = refs[:n_seq], refs[n_seq:]
    band_rows = held[0].shape[0]
    seq, tensor = place[0], place[1]
    n_tensor = order_ref.shape[0]
    pos = order_ref.shape[1]
    for i in range(count):
        order = order_ref[lax.rem(tensor + first + i, n_tensor)]
        total = None
        for d in range(n_seq):
            band = lax.rem(seq - d + n_seq, n_seq)
            pick = one_hot(
                order - band * band_rows == lax.broadcasted_iota(jnp.int32, (pos, band_rows), 1)
            )
            term = dot(pick, held[d][...])
            total = term if total is None else total + term
        outs[i][...] = total.astype(jnp.bfloat16)


def call(kernel, out_shape, n_scalar, n_vmem, flops, moved, n_hbm=0, scratch=(), limit=VMEM_LIMIT):
    return pl.pallas_call(
        kernel,
        out_shape=out_shape,
        in_specs=[SMEM] * n_scalar + [VMEM] * n_vmem + [HBM] * n_hbm,
        out_specs=jax.tree.map(lambda _: VMEM, out_shape),
        scratch_shapes=list(scratch),
        compiler_params=pltpu.CompilerParams(vmem_limit_bytes=limit),
        cost_estimate=pl.CostEstimate(flops=flops, bytes_accessed=moved, transcendentals=0),
    )


def local(
    memory_in, norm_gain, qkv_weight, out_weight, key_weight, value_weight, shift_offsets, row_order
):
    _, band_rows, emb = memory_in.shape
    n_seq = lax.axis_size("seq")
    n_tensor = lax.axis_size("tensor")
    own_cols = key_weight.shape[1] // n_seq
    pos = row_order.shape[1] // n_tensor
    rows = -(-band_rows // 16) * 16
    place = jnp.stack([lax.axis_index("seq"), lax.axis_index("tensor")]).astype(jnp.int32)
    halo = rotated(memory_in[0, : (WIN - 1) * GRID_W], "seq", -1)
    order = lax.dynamic_index_in_dim(row_order, lax.axis_index("tensor"), 0, False)
    order = order.reshape(n_tensor, pos, 1)

    rolled_own, gain, qkv_on_chip = call(
        stage_kernel,
        [
            jax.ShapeDtypeStruct((rows, emb), jnp.bfloat16),
            jax.ShapeDtypeStruct((1, emb), jnp.float32),
            jax.ShapeDtypeStruct(qkv_weight.shape, qkv_weight.dtype),
        ],
        1, 2, 50_000_000, 4_000_000, 1, [pltpu.SemaphoreType.DMA], STAGE_LIMIT,
    )(shift_offsets, memory_in, norm_gain.reshape(1, emb), qkv_weight)
    weights = [out_weight, key_weight, value_weight]
    block = jax.ShapeDtypeStruct((band_rows, own_cols), jnp.bfloat16)
    sent = call(
        functools.partial(encode_kernel, n_seq, band_rows), [block] * (2 * n_seq),
        2, 4, 2_000_000_000, 10_000_000, len(weights),
        [pltpu.VMEM(w.shape, w.dtype) for w in weights]
        + [pltpu.SemaphoreType.DMA((len(weights),))],
        ENCODE_LIMIT,
    )(place, shift_offsets, rolled_own, halo, gain, qkv_on_chip, *weights)
    key_sent, value_sent = sent[:n_seq], sent[n_seq:]

    piece = jax.ShapeDtypeStruct((pos, own_cols), jnp.bfloat16)

    def gathered(sent):
        held = [rotated(sent[d], "seq", d) if d else sent[0] for d in range(n_seq)]
        away = call(
            functools.partial(select_kernel, n_seq, 1, n_tensor - 1),
            [piece] * (n_tensor - 1), 1, 1 + n_seq, 300_000_000, 1_000_000,
        )(place, order, *held)
        arrived = [rotated(away[d - 1], "tensor", d) for d in range(1, n_tensor)]
        kept = call(
            functools.partial(select_kernel, n_seq, 0, 1),
            [piece], 1, 1 + n_seq, 300_000_000, 1_000_000,
        )(place, order, *held)
        return [*kept, *arrived]

    def by_page(blocks):
        page = jnp.arange(n_tensor)[:, None, None]
        result = blocks[0][None]
        for d in range(1, n_tensor):
            came = page == (lax.axis_index("tensor") - d) % n_tensor
            result = jnp.where(came, blocks[d][None], result)
        return jnp.broadcast_to(result, (n_tensor, pos, own_cols))

    key_out, value_blocks = lax.optimization_barrier((by_page(gathered(key_sent)), gathered(value_sent)))
    return key_out, by_page(value_blocks)


def solution(mesh):
    placed = (
        P(("dp", "tensor"), "seq", None),
        P(),
        P(),
        P(),
        P(),
        P(),
        P(("dp", "tensor"), None),
        P("dp", None),
    )
    return jax.shard_map(
        local,
        mesh=mesh,
        in_specs=placed,
        out_specs=(P("dp", "tensor", "seq"), P("dp", "tensor", "seq")),
        check_vma=False,
    )
```

```python
import functools

import jax
import jax.numpy as jnp
from jax import lax
from jax.experimental import pallas as pl
from jax.experimental.pallas import tpu as pltpu
from jax.sharding import PartitionSpec as P

HEADS = 16
HEAD_DIM = 32
GRID_H = 28
GRID_W = 21
WIN = 7

GROUP = 8
VMEM_LIMIT = 24 * 1024 * 1024

SMEM = pl.BlockSpec(memory_space=pltpu.SMEM)
VMEM = pl.BlockSpec(memory_space=pltpu.VMEM)
HBM = pl.BlockSpec(memory_space=pltpu.HBM)


def rotated(block, axis, distance):
    devices = lax.axis_size(axis)
    return lax.ppermute(block, axis, [(i, (i + distance) % devices) for i in range(devices)])


def paired(n):
    return n & (n - 1) == 0


def target(place, d, n):
    return place ^ d if paired(n) else lax.rem(place + d, n)


def origin(place, d, n):
    return place ^ d if paired(n) else lax.rem(place - d + n, n)


def exchanged(block, axis, d):
    n = lax.axis_size(axis)
    pairs = [(i, i ^ d if paired(n) else (i + d) % n) for i in range(n)]
    return lax.ppermute(block, axis, pairs)


def band_of(seq, n_seq):
    return lax.rem(seq + n_seq - 1, n_seq)


def dot(a, b):
    return jnp.dot(a, b, preferred_element_type=jnp.float32)


def one_hot(cond):
    return jnp.where(cond, 1.0, 0.0).astype(jnp.bfloat16)


def stage_kernel(n_seq, place, shifts_hbm, pages_hbm, gain_hbm, *refs):
    weights, refs = refs[:4], refs[4:]
    rolled_ref, take_ref, same_ref, gain_ref, *staged = refs[:8]
    shifts, own, arrived = refs[8:]
    pairs = [(shifts_hbm, shifts), (pages_hbm.at[0], own), (gain_hbm, gain_ref)]
    pairs += list(zip(weights, staged))
    copies = [pltpu.make_async_copy(*pair, arrived.at[i]) for i, pair in enumerate(pairs)]
    for copy in copies:
        copy.start()
    band_rows = own.shape[0]
    rows, halo_rows = take_ref.shape
    copies[0].wait()
    row_shift, col_shift = shifts[0, 0], shifts[0, 1]

    cell = lax.broadcasted_iota(jnp.int32, (rows, 1), 0)
    cell_row = cell // GRID_W
    from_col = cell - cell_row * GRID_W + col_shift
    from_col = jnp.where(from_col >= GRID_W, from_col - GRID_W, from_col)
    skipped = band_rows - halo_rows
    source = jnp.where(cell < band_rows, (cell_row + row_shift) * GRID_W + from_col - skipped, -1)
    take_ref[...] = one_hot(source == lax.broadcasted_iota(jnp.int32, (rows, halo_rows), 1))
    take_own = one_hot(
        source - halo_rows == lax.broadcasted_iota(jnp.int32, (rows, band_rows), 1)
    )

    band = band_of(place[0], n_seq)

    def marks(index):
        row = index // GRID_W
        col = index - row * GRID_W
        wrap_row = (band * WIN + row >= GRID_H - row_shift).astype(jnp.int32)
        wrap_col = (col >= GRID_W - col_shift).astype(jnp.int32)
        return jnp.where(index < band_rows, (col // WIN) * 4 + 2 * wrap_row + wrap_col, -1)

    same = marks(cell) == marks(lax.broadcasted_iota(jnp.int32, (1, rows), 1))
    same_ref[...] = same.astype(jnp.int32)
    copies[1].wait()
    rolled_ref[...] = dot(take_own, own[...]).astype(jnp.bfloat16)
    for copy in copies[2:]:
        copy.wait()


def encode_kernel(
    n_seq, place, rolled_ref, halo_ref, take_ref, same_ref, gain_ref, qkv_ref, out_ref, key_ref,
    value_ref, *sent
):
    rows = rolled_ref.shape[0]
    attn = HEADS * HEAD_DIM
    seq = place[0]
    rolled = rolled_ref[...].astype(jnp.float32) + dot(take_ref[...], halo_ref[...])

    mean = jnp.mean(rolled, axis=-1, keepdims=True)
    centred = rolled - mean
    variance = jnp.mean(centred * centred, axis=-1, keepdims=True)
    normed = (centred * lax.rsqrt(variance + 1e-05) * gain_ref[...]).astype(jnp.bfloat16)
    qkv = dot(normed, qkv_ref[...]).astype(jnp.bfloat16)
    queries, keys, values = (qkv[:, i * attn : (i + 1) * attn] for i in range(3))

    same = jnp.concatenate([same_ref[...]] * GROUP, axis=0) != 0
    width = GROUP * HEAD_DIM
    lane_head = lax.broadcasted_iota(jnp.int32, (1, width), 1) // HEAD_DIM
    parts = []
    for g in range(HEADS // GROUP):
        at = g * width
        q, k, v = (part[:, at : at + width] for part in (queries, keys, values))
        stacked = jnp.concatenate(
            [jnp.where(lane_head == h, q, jnp.zeros_like(q)) for h in range(GROUP)], axis=0
        )
        scores = lax.dot_general(
            stacked, k, (((1,), (1,)), ((), ())), preferred_element_type=jnp.float32
        )
        scores = jnp.where(same, scores * HEAD_DIM ** (-0.5), -1000000000.0)
        scores = jnp.exp(scores - jnp.max(scores, axis=-1, keepdims=True))
        total = jnp.sum(scores, axis=-1, keepdims=True)
        weights = (scores * (1.0 / total)).astype(jnp.bfloat16)
        mixed = dot(weights, v)
        part = jnp.zeros((rows, width), jnp.float32)
        for h in range(GROUP):
            part = jnp.where(lane_head == h, mixed[h * rows : (h + 1) * rows], part)
        parts.append(part.astype(jnp.bfloat16))
    attended = jnp.concatenate(parts, axis=1)
    memory = (rolled + dot(attended, out_ref[...])).astype(jnp.bfloat16)

    own_cols = key_ref.shape[1] // n_seq
    for weight_ref, blocks in ((key_ref, sent[:n_seq]), (value_ref, sent[n_seq:])):
        for d in range(n_seq):
            cols = pl.ds(pl.multiple_of(target(seq, d, n_seq) * own_cols, own_cols), own_cols)
            block = dot(memory, weight_ref[:, cols])
            blocks[d][...] = block[: blocks[d].shape[0]].astype(jnp.bfloat16)


def select_kernel(rounds, first, count, place, order_ref, *refs):
    n_seq = len(rounds)
    held, outs = refs[:n_seq], refs[n_seq:]
    band_rows = held[0].shape[0]
    seq, tensor = place[0], place[1]
    n_tensor = order_ref.shape[0]
    pos = order_ref.shape[1]
    for i in range(count):
        order = order_ref[lax.rem(tensor + first + i, n_tensor)]
        total = None
        for d, block in zip(rounds, held):
            band = band_of(origin(seq, d, n_seq), n_seq)
            pick = one_hot(
                order - band * band_rows == lax.broadcasted_iota(jnp.int32, (pos, band_rows), 1)
            )
            term = dot(pick, block[...])
            total = term if total is None else total + term
        outs[i][...] = total.astype(jnp.bfloat16)


def call(kernel, out_shape, n_scalar, n_vmem, flops, moved, n_hbm=0, scratch=()):
    return pl.pallas_call(
        kernel,
        out_shape=out_shape,
        in_specs=[SMEM] * n_scalar + [VMEM] * n_vmem + [HBM] * n_hbm,
        out_specs=jax.tree.map(lambda _: VMEM, out_shape),
        scratch_shapes=list(scratch),
        compiler_params=pltpu.CompilerParams(vmem_limit_bytes=VMEM_LIMIT),
        cost_estimate=pl.CostEstimate(flops=flops, bytes_accessed=moved, transcendentals=0),
    )


def local(
    memory_in, norm_gain, qkv_weight, out_weight, key_weight, value_weight, shift_offsets, row_order
):
    _, band_rows, emb = memory_in.shape
    n_seq = lax.axis_size("seq")
    n_tensor = lax.axis_size("tensor")
    own_cols = key_weight.shape[1] // n_seq
    pos = row_order.shape[1] // n_tensor
    rows = -(-band_rows // 16) * 16
    place = jnp.stack([lax.axis_index("seq"), lax.axis_index("tensor")]).astype(jnp.int32)
    halo = rotated(memory_in[0, GRID_W :], "seq", 1)
    order = lax.dynamic_index_in_dim(row_order, lax.axis_index("tensor"), 0, False)
    order = order.reshape(n_tensor, pos, 1)

    weights = [qkv_weight, out_weight, key_weight, value_weight]
    off_chip = [shift_offsets, memory_in, norm_gain.reshape(1, emb), *weights]
    staged = call(
        functools.partial(stage_kernel, n_seq),
        [
            jax.ShapeDtypeStruct((rows, emb), jnp.bfloat16),
            jax.ShapeDtypeStruct((rows, halo.shape[0]), jnp.bfloat16),
            jax.ShapeDtypeStruct((rows, rows), jnp.int32),
            jax.ShapeDtypeStruct((1, emb), jnp.float32),
        ]
        + [jax.ShapeDtypeStruct(w.shape, w.dtype) for w in weights],
        1, 0, 50_000_000, 8_000_000, len(off_chip),
        [
            pltpu.SMEM(shift_offsets.shape, jnp.int32),
            pltpu.VMEM((band_rows, emb), jnp.bfloat16),
            pltpu.SemaphoreType.DMA((len(off_chip),)),
        ],
    )(place, *(pltpu.with_memory_space_constraint(x, pltpu.HBM) for x in off_chip))
    block = jax.ShapeDtypeStruct((band_rows, own_cols), jnp.bfloat16)
    sent = call(
        functools.partial(encode_kernel, n_seq), [block] * (2 * n_seq),
        1, 9, 2_000_000_000, 10_000_000,
    )(place, staged[0], halo, *staged[1:])

    rounds = [*range(2, n_seq), 1]
    key_held = [sent[0]] + [exchanged(sent[d], "seq", d) for d in rounds]
    value_held = [sent[n_seq]] + [exchanged(sent[n_seq + d], "seq", d) for d in rounds]

    piece = jax.ShapeDtypeStruct((pos, own_cols), jnp.bfloat16)

    def gathered(held):
        away = call(
            functools.partial(select_kernel, [0, *rounds], 1, n_tensor - 1),
            [piece] * (n_tensor - 1), 1, 1 + n_seq, 300_000_000, 1_000_000,
        )(place, order, *held)
        arrived = [rotated(away[d - 1], "tensor", d) for d in range(1, n_tensor)]
        kept = call(
            functools.partial(select_kernel, [0, *rounds], 0, 1),
            [piece], 1, 1 + n_seq, 300_000_000, 1_000_000,
        )(place, order, *held)
        return [*kept, *arrived]

    def by_page(blocks):
        page = jnp.arange(n_tensor)[:, None, None]
        result = blocks[0][None]
        for d in range(1, n_tensor):
            came = page == (lax.axis_index("tensor") - d) % n_tensor
            result = jnp.where(came, blocks[d][None], result)
        return jnp.broadcast_to(result, (n_tensor, pos, own_cols))

    key_out, value_blocks = lax.optimization_barrier(
        (by_page(gathered(key_held)), gathered(value_held))
    )
    return key_out, by_page(value_blocks)


def solution(mesh):
    placed = (
        P(("dp", "tensor"), "seq", None),
        P(),
        P(),
        P(),
        P(),
        P(),
        P(("dp", "tensor"), None),
        P("dp", None),
    )
    return jax.shard_map(
        local,
        mesh=mesh,
        in_specs=placed,
        out_specs=(P("dp", "tensor", "seq"), P("dp", "tensor", "seq")),
        check_vma=False,
    )
```

```python
import functools

import jax
import jax.numpy as jnp
from jax import lax
from jax.experimental import pallas as pl
from jax.experimental.pallas import tpu as pltpu
from jax.sharding import PartitionSpec as P

HEADS = 16
HEAD_DIM = 32
GRID_H = 28
GRID_W = 21
WIN = 7

GROUP = 8
VMEM_LIMIT = 24 * 1024 * 1024

SMEM = pl.BlockSpec(memory_space=pltpu.SMEM)
VMEM = pl.BlockSpec(memory_space=pltpu.VMEM)
HBM = pl.BlockSpec(memory_space=pltpu.HBM)


def rotated(block, axis, distance):
    devices = lax.axis_size(axis)
    return lax.ppermute(block, axis, [(i, (i + distance) % devices) for i in range(devices)])


def paired(n):
    return n & (n - 1) == 0


def target(place, d, n):
    return place ^ d if paired(n) else lax.rem(place + d, n)


def origin(place, d, n):
    return place ^ d if paired(n) else lax.rem(place - d + n, n)


def exchanged(block, axis, d):
    n = lax.axis_size(axis)
    pairs = [(i, i ^ d if paired(n) else (i + d) % n) for i in range(n)]
    return lax.ppermute(block, axis, pairs)


def band_of(seq, n_seq):
    return lax.rem(seq + n_seq - 1, n_seq)


def dot(a, b):
    return jnp.dot(a, b, preferred_element_type=jnp.float32)


def one_hot(cond):
    return jnp.where(cond, 1.0, 0.0).astype(jnp.bfloat16)


def stage_kernel(rounds, place, order_ref, shifts_hbm, pages_hbm, gain_hbm, *refs):
    weights, refs = refs[:4], refs[4:]
    rolled_ref, take_ref, same_ref, picks_ref, gain_ref, *staged = refs[:9]
    shifts, own, arrived = refs[9:]
    pairs = [(shifts_hbm, shifts), (pages_hbm.at[0], own), (gain_hbm, gain_ref)]
    pairs += list(zip(weights, staged))
    copies = [pltpu.make_async_copy(*pair, arrived.at[i]) for i, pair in enumerate(pairs)]
    for copy in copies:
        copy.start()
    band_rows = own.shape[0]
    rows, halo_rows = take_ref.shape
    n_seq = len(rounds)
    n_tensor, pos, _ = order_ref.shape
    for i in range(n_tensor):
        order = order_ref[lax.rem(place[1] + i, n_tensor)]
        for r, d in enumerate(rounds):
            local = order - band_of(origin(place[0], d, n_seq), n_seq) * band_rows
            picks_ref[i, r] = one_hot(
                local == lax.broadcasted_iota(jnp.int32, (pos, band_rows), 1)
            )
    copies[0].wait()
    row_shift, col_shift = shifts[0, 0], shifts[0, 1]

    cell = lax.broadcasted_iota(jnp.int32, (rows, 1), 0)
    cell_row = cell // GRID_W
    from_col = cell - cell_row * GRID_W + col_shift
    from_col = jnp.where(from_col >= GRID_W, from_col - GRID_W, from_col)
    skipped = band_rows - halo_rows
    source = jnp.where(cell < band_rows, (cell_row + row_shift) * GRID_W + from_col - skipped, -1)
    take_ref[...] = one_hot(source == lax.broadcasted_iota(jnp.int32, (rows, halo_rows), 1))
    take_own = one_hot(
        source - halo_rows == lax.broadcasted_iota(jnp.int32, (rows, band_rows), 1)
    )

    band = band_of(place[0], n_seq)

    def marks(index):
        row = index // GRID_W
        col = index - row * GRID_W
        wrap_row = (band * WIN + row >= GRID_H - row_shift).astype(jnp.int32)
        wrap_col = (col >= GRID_W - col_shift).astype(jnp.int32)
        return jnp.where(index < band_rows, (col // WIN) * 4 + 2 * wrap_row + wrap_col, -1)

    same = marks(cell) == marks(lax.broadcasted_iota(jnp.int32, (1, rows), 1))
    same_ref[...] = same.astype(jnp.int32)
    copies[1].wait()
    rolled_ref[...] = dot(take_own, own[...]).astype(jnp.bfloat16)
    for copy in copies[2:]:
        copy.wait()


def encode_kernel(
    blocks, place, rolled_ref, halo_ref, take_ref, same_ref, gain_ref, qkv_ref, out_ref, key_ref,
    value_ref, *sent
):
    rows = rolled_ref.shape[0]
    attn = HEADS * HEAD_DIM
    rolled = rolled_ref[...].astype(jnp.float32) + dot(take_ref[...], halo_ref[...])

    mean = jnp.mean(rolled, axis=-1, keepdims=True)
    centred = rolled - mean
    variance = jnp.mean(centred * centred, axis=-1, keepdims=True)
    normed = (centred * lax.rsqrt(variance + 1e-05) * gain_ref[...]).astype(jnp.bfloat16)
    qkv = dot(normed, qkv_ref[...]).astype(jnp.bfloat16)
    queries, keys, values = (qkv[:, i * attn : (i + 1) * attn] for i in range(3))

    same = jnp.concatenate([same_ref[...]] * GROUP, axis=0) != 0
    width = GROUP * HEAD_DIM
    lane_head = lax.broadcasted_iota(jnp.int32, (1, width), 1) // HEAD_DIM
    parts = []
    for g in range(HEADS // GROUP):
        at = g * width
        q, k, v = (part[:, at : at + width] for part in (queries, keys, values))
        stacked = jnp.concatenate(
            [jnp.where(lane_head == h, q, jnp.zeros_like(q)) for h in range(GROUP)], axis=0
        )
        scores = lax.dot_general(
            stacked, k, (((1,), (1,)), ((), ())), preferred_element_type=jnp.float32
        )
        scores = jnp.where(same, scores * HEAD_DIM ** (-0.5), -1000000000.0)
        scores = jnp.exp(scores - jnp.max(scores, axis=-1, keepdims=True))
        total = jnp.sum(scores, axis=-1, keepdims=True)
        weights = (scores * (1.0 / total)).astype(jnp.bfloat16)
        mixed = dot(weights, v)
        part = jnp.zeros((rows, width), jnp.float32)
        for h in range(GROUP):
            part = jnp.where(lane_head == h, mixed[h * rows : (h + 1) * rows], part)
        parts.append(part.astype(jnp.bfloat16))
    attended = jnp.concatenate(parts, axis=1)
    memory = (rolled + dot(attended, out_ref[...])).astype(jnp.bfloat16)
    own_cols = sent[0].shape[1]
    for (is_value, d), block_ref in zip(blocks, sent):
        at = target(place[0], d, key_ref.shape[1] // own_cols) * own_cols
        weight_ref = value_ref if is_value else key_ref
        block = dot(memory, weight_ref[:, pl.ds(pl.multiple_of(at, own_cols), own_cols)])
        block_ref[...] = block[: block_ref.shape[0]].astype(jnp.bfloat16)


def select_kernel(n_seq, first, picks_ref, *refs):
    held, outs = refs[:n_seq], refs[n_seq:]
    for i, out in enumerate(outs):
        terms = [dot(picks_ref[first + i, r], held[r][...]) for r in range(n_seq)]
        out[...] = sum(terms[1:], terms[0]).astype(jnp.bfloat16)


def call(kernel, out_shape, n_scalar, n_vmem, flops, moved, n_hbm=0, scratch=()):
    return pl.pallas_call(
        kernel,
        out_shape=out_shape,
        in_specs=[SMEM] * n_scalar + [VMEM] * n_vmem + [HBM] * n_hbm,
        out_specs=jax.tree.map(lambda _: VMEM, out_shape),
        scratch_shapes=list(scratch),
        compiler_params=pltpu.CompilerParams(vmem_limit_bytes=VMEM_LIMIT),
        cost_estimate=pl.CostEstimate(flops=flops, bytes_accessed=moved, transcendentals=0),
    )


def local(
    memory_in, norm_gain, qkv_weight, out_weight, key_weight, value_weight, shift_offsets, row_order
):
    _, band_rows, emb = memory_in.shape
    n_seq = lax.axis_size("seq")
    n_tensor = lax.axis_size("tensor")
    own_cols = key_weight.shape[1] // n_seq
    pos = row_order.shape[1] // n_tensor
    rows = -(-band_rows // 16) * 16
    place = jnp.stack([lax.axis_index("seq"), lax.axis_index("tensor")]).astype(jnp.int32)
    halo = rotated(memory_in[0, GRID_W :], "seq", 1)
    order = lax.dynamic_index_in_dim(row_order, lax.axis_index("tensor"), 0, False)
    order = order.reshape(n_tensor, pos, 1)

    rounds = [*range(2, n_seq), 1, 0]
    weights = [qkv_weight, out_weight, key_weight, value_weight]
    off_chip = [shift_offsets, memory_in, norm_gain.reshape(1, emb), *weights]
    rolled_own, take, same, picks, gain, qkv_chip, out_chip, key_chip, value_chip = call(
        functools.partial(stage_kernel, rounds),
        [
            jax.ShapeDtypeStruct((rows, emb), jnp.bfloat16),
            jax.ShapeDtypeStruct((rows, halo.shape[0]), jnp.bfloat16),
            jax.ShapeDtypeStruct((rows, rows), jnp.int32),
            jax.ShapeDtypeStruct((n_tensor, n_seq, pos, band_rows), jnp.bfloat16),
            jax.ShapeDtypeStruct((1, emb), jnp.float32),
        ]
        + [jax.ShapeDtypeStruct(w.shape, w.dtype) for w in weights],
        1, 1, 50_000_000, 8_000_000, len(off_chip),
        [
            pltpu.SMEM(shift_offsets.shape, jnp.int32),
            pltpu.VMEM((band_rows, emb), jnp.bfloat16),
            pltpu.SemaphoreType.DMA((len(off_chip),)),
        ],
    )(place, order, *(pltpu.with_memory_space_constraint(x, pltpu.HBM) for x in off_chip))

    block = jax.ShapeDtypeStruct((band_rows, own_cols), jnp.bfloat16)
    blocks = [(is_value, d) for is_value in (False, True) for d in rounds]
    sent = call(
        functools.partial(encode_kernel, blocks), [block] * len(blocks),
        1, 9, 2_000_000_000, 10_000_000,
    )(place, rolled_own, halo, take, same, gain, qkv_chip, out_chip, key_chip, value_chip)
    held = [exchanged(b, "seq", d) if d else b for (_, d), b in zip(blocks, sent)]

    def selected(group, first, count):
        return call(
            functools.partial(select_kernel, n_seq, first),
            [jax.ShapeDtypeStruct((pos, own_cols), jnp.bfloat16)] * count,
            0, 1 + n_seq, 300_000_000, 1_000_000,
        )(picks, *held[group * n_seq : (group + 1) * n_seq])

    def gathered(group):
        away = selected(group, 1, n_tensor - 1)
        arrived = [rotated(away[d - 1], "tensor", d) for d in range(1, n_tensor)]
        return [*selected(group, 0, 1), *arrived]

    def by_page(blocks):
        page = jnp.arange(n_tensor)[:, None, None]
        result = blocks[0][None]
        for d in range(1, n_tensor):
            came = page == (lax.axis_index("tensor") - d) % n_tensor
            result = jnp.where(came, blocks[d][None], result)
        return jnp.broadcast_to(result, (n_tensor, pos, own_cols))

    key_out, value_blocks = lax.optimization_barrier((by_page(gathered(0)), gathered(1)))
    return key_out, by_page(value_blocks)


def solution(mesh):
    placed = (
        P(("dp", "tensor"), "seq", None),
        P(),
        P(),
        P(),
        P(),
        P(),
        P(("dp", "tensor"), None),
        P("dp", None),
    )
    return jax.shard_map(
        local,
        mesh=mesh,
        in_specs=placed,
        out_specs=(P("dp", "tensor", "seq"), P("dp", "tensor", "seq")),
        check_vma=False,
    )
```

```python
import functools

import jax
import jax.numpy as jnp
from jax import lax
from jax.experimental import pallas as pl
from jax.experimental.pallas import tpu as pltpu
from jax.sharding import PartitionSpec as P

HEADS = 16
HEAD_DIM = 32
GRID_H = 28
GRID_W = 21
WIN = 7

GROUP = 8
VMEM_LIMIT = 24 * 1024 * 1024

SMEM = pl.BlockSpec(memory_space=pltpu.SMEM)
VMEM = pl.BlockSpec(memory_space=pltpu.VMEM)
HBM = pl.BlockSpec(memory_space=pltpu.HBM)


def rotated(block, axis, distance):
    devices = lax.axis_size(axis)
    return lax.ppermute(block, axis, [(i, (i + distance) % devices) for i in range(devices)])


def paired(n):
    return n & (n - 1) == 0


def rounds_of(n):
    return [(0, 0)] + list(zip([1, *range(2, n)], [*range(2, n), 1]))


def distance(place, r, n):
    even, odd = rounds_of(n)[r]
    return jnp.where(lax.rem(place[2], 2) == 0, even, odd)


def target(place, r, n):
    d = distance(place, r, n)
    return place[0] ^ d if paired(n) else lax.rem(place[0] + d, n)


def origin(place, r, n):
    d = distance(place, r, n)
    return place[0] ^ d if paired(n) else lax.rem(place[0] - d + n, n)


def exchanged(block, r):
    n = lax.axis_size("seq")
    pairs = []
    for i in range(lax.axis_size("dp")):
        d = rounds_of(n)[r][i % 2]
        pairs += [(i * n + j, i * n + (j ^ d if paired(n) else (j + d) % n)) for j in range(n)]
    return lax.ppermute(block, ("dp", "seq"), pairs)


def band_of(seq, n_seq):
    return lax.rem(seq + n_seq - 1, n_seq)


def dot(a, b):
    return jnp.dot(a, b, preferred_element_type=jnp.float32)


def one_hot(cond):
    return jnp.where(cond, 1.0, 0.0).astype(jnp.bfloat16)


def stage_kernel(place, order_ref, shifts_hbm, pages_hbm, gain_hbm, *refs):
    weights, refs = refs[:4], refs[4:]
    rolled_ref, take_ref, same_ref, picks_ref, gain_ref, *staged = refs[:9]
    shifts, own, arrived = refs[9:]
    pairs = [(shifts_hbm, shifts), (pages_hbm.at[0], own), (gain_hbm, gain_ref)]
    pairs += list(zip(weights, staged))
    copies = [pltpu.make_async_copy(*pair, arrived.at[i]) for i, pair in enumerate(pairs)]
    for copy in copies:
        copy.start()
    band_rows = own.shape[0]
    rows, halo_rows = take_ref.shape
    n_tensor, n_seq, pos, _ = picks_ref.shape
    for i in range(n_tensor):
        order = order_ref[lax.rem(place[1] + i, n_tensor)]
        for r in range(n_seq):
            local = order - band_of(origin(place, r, n_seq), n_seq) * band_rows
            picks_ref[i, r] = one_hot(
                local == lax.broadcasted_iota(jnp.int32, (pos, band_rows), 1)
            )
    copies[0].wait()
    row_shift, col_shift = shifts[0, 0], shifts[0, 1]

    cell = lax.broadcasted_iota(jnp.int32, (rows, 1), 0)
    cell_row = cell // GRID_W
    from_col = cell - cell_row * GRID_W + col_shift
    from_col = jnp.where(from_col >= GRID_W, from_col - GRID_W, from_col)
    skipped = band_rows - halo_rows
    source = jnp.where(cell < band_rows, (cell_row + row_shift) * GRID_W + from_col - skipped, -1)
    take_ref[...] = one_hot(source == lax.broadcasted_iota(jnp.int32, (rows, halo_rows), 1))
    take_own = one_hot(
        source - halo_rows == lax.broadcasted_iota(jnp.int32, (rows, band_rows), 1)
    )

    band = band_of(place[0], n_seq)

    def marks(index):
        row = index // GRID_W
        col = index - row * GRID_W
        wrap_row = (band * WIN + row >= GRID_H - row_shift).astype(jnp.int32)
        wrap_col = (col >= GRID_W - col_shift).astype(jnp.int32)
        return jnp.where(index < band_rows, (col // WIN) * 4 + 2 * wrap_row + wrap_col, -1)

    same = marks(cell) == marks(lax.broadcasted_iota(jnp.int32, (1, rows), 1))
    same_ref[...] = same.astype(jnp.int32)
    copies[1].wait()
    rolled_ref[...] = dot(take_own, own[...]).astype(jnp.bfloat16)
    for copy in copies[2:]:
        copy.wait()


def encode_kernel(
    blocks, place, rolled_ref, halo_ref, take_ref, same_ref, gain_ref, qkv_ref, out_ref, key_ref,
    value_ref, *sent
):
    rows = rolled_ref.shape[0]
    attn = HEADS * HEAD_DIM
    rolled = rolled_ref[...].astype(jnp.float32) + dot(take_ref[...], halo_ref[...])

    mean = jnp.mean(rolled, axis=-1, keepdims=True)
    centred = rolled - mean
    variance = jnp.mean(centred * centred, axis=-1, keepdims=True)
    normed = (centred * lax.rsqrt(variance + 1e-05) * gain_ref[...]).astype(jnp.bfloat16)
    qkv = dot(normed, qkv_ref[...]).astype(jnp.bfloat16)
    queries, keys, values = (qkv[:, i * attn : (i + 1) * attn] for i in range(3))

    same = jnp.concatenate([same_ref[...]] * GROUP, axis=0) != 0
    width = GROUP * HEAD_DIM
    lane_head = lax.broadcasted_iota(jnp.int32, (1, width), 1) // HEAD_DIM
    parts = []
    for g in range(HEADS // GROUP):
        at = g * width
        q, k, v = (part[:, at : at + width] for part in (queries, keys, values))
        stacked = jnp.concatenate(
            [jnp.where(lane_head == h, q, jnp.zeros_like(q)) for h in range(GROUP)], axis=0
        )
        scores = lax.dot_general(
            stacked, k, (((1,), (1,)), ((), ())), preferred_element_type=jnp.float32
        )
        scores = jnp.where(same, scores * HEAD_DIM ** (-0.5), -1000000000.0)
        scores = jnp.exp(scores - jnp.max(scores, axis=-1, keepdims=True))
        total = jnp.sum(scores, axis=-1, keepdims=True)
        weights = (scores * (1.0 / total)).astype(jnp.bfloat16)
        mixed = dot(weights, v)
        part = jnp.zeros((rows, width), jnp.float32)
        for h in range(GROUP):
            part = jnp.where(lane_head == h, mixed[h * rows : (h + 1) * rows], part)
        parts.append(part.astype(jnp.bfloat16))
    attended = jnp.concatenate(parts, axis=1)
    memory = (rolled + dot(attended, out_ref[...])).astype(jnp.bfloat16)
    own_cols = sent[0].shape[1]
    for (is_value, r), block_ref in zip(blocks, sent):
        at = target(place, r, key_ref.shape[1] // own_cols) * own_cols
        weight_ref = value_ref if is_value else key_ref
        block = dot(memory, weight_ref[:, pl.ds(pl.multiple_of(at, own_cols), own_cols)])
        block_ref[...] = block[: block_ref.shape[0]].astype(jnp.bfloat16)


def select_kernel(n_seq, first, picks_ref, *refs):
    held, outs = refs[:n_seq], refs[n_seq:]
    for i, out in enumerate(outs):
        terms = [dot(picks_ref[first + i, r], held[r][...]) for r in range(n_seq)]
        out[...] = sum(terms[1:], terms[0]).astype(jnp.bfloat16)


def call(kernel, out_shape, n_scalar, n_vmem, flops, moved, n_hbm=0, scratch=()):
    return pl.pallas_call(
        kernel,
        out_shape=out_shape,
        in_specs=[SMEM] * n_scalar + [VMEM] * n_vmem + [HBM] * n_hbm,
        out_specs=jax.tree.map(lambda _: VMEM, out_shape),
        scratch_shapes=list(scratch),
        compiler_params=pltpu.CompilerParams(vmem_limit_bytes=VMEM_LIMIT),
        cost_estimate=pl.CostEstimate(flops=flops, bytes_accessed=moved, transcendentals=0),
    )


def local(
    memory_in, norm_gain, qkv_weight, out_weight, key_weight, value_weight, shift_offsets, row_order
):
    _, band_rows, emb = memory_in.shape
    n_seq = lax.axis_size("seq")
    n_tensor = lax.axis_size("tensor")
    own_cols = key_weight.shape[1] // n_seq
    pos = row_order.shape[1] // n_tensor
    rows = -(-band_rows // 16) * 16
    place = jnp.stack([lax.axis_index(axis) for axis in ("seq", "tensor", "dp")]).astype(jnp.int32)
    halo = rotated(memory_in[0, GRID_W :], "seq", 1)
    order = lax.dynamic_index_in_dim(row_order, lax.axis_index("tensor"), 0, False)
    order = order.reshape(n_tensor, pos, 1)

    weights = [qkv_weight, out_weight, key_weight, value_weight]
    off_chip = [shift_offsets, memory_in, norm_gain.reshape(1, emb), *weights]
    rolled_own, take, same, picks, gain, qkv_chip, out_chip, key_chip, value_chip = call(
        stage_kernel,
        [
            jax.ShapeDtypeStruct((rows, emb), jnp.bfloat16),
            jax.ShapeDtypeStruct((rows, halo.shape[0]), jnp.bfloat16),
            jax.ShapeDtypeStruct((rows, rows), jnp.int32),
            jax.ShapeDtypeStruct((n_tensor, n_seq, pos, band_rows), jnp.bfloat16),
            jax.ShapeDtypeStruct((1, emb), jnp.float32),
        ]
        + [jax.ShapeDtypeStruct(w.shape, w.dtype) for w in weights],
        1, 1, 50_000_000, 8_000_000, len(off_chip),
        [
            pltpu.SMEM(shift_offsets.shape, jnp.int32),
            pltpu.VMEM((band_rows, emb), jnp.bfloat16),
            pltpu.SemaphoreType.DMA((len(off_chip),)),
        ],
    )(place, order, *(pltpu.with_memory_space_constraint(x, pltpu.HBM) for x in off_chip))

    block = jax.ShapeDtypeStruct((band_rows, own_cols), jnp.bfloat16)
    blocks = [(is_value, r) for is_value in (False, True) for r in range(n_seq)]
    sent = call(
        functools.partial(encode_kernel, blocks), [block] * len(blocks),
        1, 9, 2_000_000_000, 10_000_000,
    )(place, rolled_own, halo, take, same, gain, qkv_chip, out_chip, key_chip, value_chip)
    held = [exchanged(b, r) if r else b for (_, r), b in zip(blocks, sent)]

    def selected(group, first, count):
        return call(
            functools.partial(select_kernel, n_seq, first),
            [jax.ShapeDtypeStruct((pos, own_cols), jnp.bfloat16)] * count,
            0, 1 + n_seq, 300_000_000, 1_000_000,
        )(picks, *held[group * n_seq : (group + 1) * n_seq])

    def gathered(group):
        away = selected(group, 1, n_tensor - 1)
        arrived = [rotated(away[d - 1], "tensor", d) for d in range(1, n_tensor)]
        return [*selected(group, 0, 1), *arrived]

    def by_page(blocks):
        page = jnp.arange(n_tensor)[:, None, None]
        result = blocks[0][None]
        for d in range(1, n_tensor):
            came = page == (lax.axis_index("tensor") - d) % n_tensor
            result = jnp.where(came, blocks[d][None], result)
        return jnp.broadcast_to(result, (n_tensor, pos, own_cols))

    key_out, value_blocks = lax.optimization_barrier((by_page(gathered(0)), gathered(1)))
    return key_out, by_page(value_blocks)


def solution(mesh):
    placed = (
        P(("dp", "tensor"), "seq", None),
        P(),
        P(),
        P(),
        P(),
        P(),
        P(("dp", "tensor"), None),
        P("dp", None),
    )
    return jax.shard_map(
        local,
        mesh=mesh,
        in_specs=placed,
        out_specs=(P("dp", "tensor", "seq"), P("dp", "tensor", "seq")),
        check_vma=False,
    )
```

```python
import functools

import jax
import jax.numpy as jnp
from jax import lax
from jax.experimental import pallas as pl
from jax.experimental.pallas import tpu as pltpu
from jax.sharding import PartitionSpec as P

HEADS = 16
HEAD_DIM = 32
GRID_H = 28
GRID_W = 21
WIN = 7

GROUP = 8
SLAB = (56, 64)
VMEM_LIMIT = 24 * 1024 * 1024

SMEM = pl.BlockSpec(memory_space=pltpu.SMEM)
VMEM = pl.BlockSpec(memory_space=pltpu.VMEM)
HBM = pl.BlockSpec(memory_space=pltpu.HBM)


def rotated(block, axis, distance):
    devices = lax.axis_size(axis)
    return lax.ppermute(block, axis, [(i, (i + distance) % devices) for i in range(devices)])


def paired(n):
    return n & (n - 1) == 0


def rounds_of(n):
    return [(0, 0)] + list(zip([1, *range(2, n)], [*range(2, n), 1]))


def distance(place, r, n):
    even, odd = rounds_of(n)[r]
    return jnp.where(lax.rem(place[2], 2) == 0, even, odd)


def target(place, r, n):
    d = distance(place, r, n)
    return place[0] ^ d if paired(n) else lax.rem(place[0] + d, n)


def origin(place, r, n):
    d = distance(place, r, n)
    return place[0] ^ d if paired(n) else lax.rem(place[0] - d + n, n)


def exchanged(block, r):
    n = lax.axis_size("seq")
    pairs = []
    for i in range(lax.axis_size("dp")):
        d = rounds_of(n)[r][i % 2]
        pairs += [(i * n + j, i * n + (j ^ d if paired(n) else (j + d) % n)) for j in range(n)]
    return lax.ppermute(block, ("dp", "seq"), pairs)


def band_of(seq, n_seq):
    return lax.rem(seq + n_seq - 1, n_seq)


def dot(a, b):
    return jnp.dot(a, b, preferred_element_type=jnp.float32)


def one_hot(cond):
    return jnp.where(cond, 1.0, 0.0).astype(jnp.bfloat16)


def cells(index, band_rows):
    window = index // (WIN * WIN)
    inside = index - window * (WIN * WIN)
    row = inside // WIN
    return row, window * WIN + inside - row * WIN


def slab(window):
    return window * WIN * WIN // 8 * 8


def stage_kernel(place, order_ref, shifts_hbm, pages_hbm, gain_hbm, *refs):
    weights, refs = refs[:4], refs[4:]
    rolled_ref, take_ref, same_ref, picks_ref, gain_ref, *staged = refs[:9]
    shifts, own, arrived = refs[9:]
    pairs = [(shifts_hbm, shifts), (pages_hbm.at[0], own), (gain_hbm, gain_ref)]
    pairs += list(zip(weights, staged))
    copies = [pltpu.make_async_copy(*pair, arrived.at[i]) for i, pair in enumerate(pairs)]
    for copy in copies:
        copy.start()
    band_rows = own.shape[0]
    rows, halo_rows = take_ref.shape
    n_tensor, n_seq, pos, _ = picks_ref.shape
    for i in range(n_tensor):
        order = order_ref[lax.rem(place[1] + i, n_tensor)]
        order_band = order // band_rows
        row = (order - order_band * band_rows) // GRID_W
        col = order - order_band * band_rows - row * GRID_W
        window = col // WIN
        cell_at = (window * WIN + row) * WIN + col - window * WIN
        for r in range(n_seq):
            band = band_of(origin(place, r, n_seq), n_seq)
            at = jnp.where(order_band == band, cell_at, -1)
            picks_ref[i, r] = one_hot(at == lax.broadcasted_iota(jnp.int32, (1, band_rows), 1))
    copies[0].wait()
    row_shift, col_shift = shifts[0, 0], shifts[0, 1]

    cell = lax.broadcasted_iota(jnp.int32, (rows, 1), 0)
    cell_row, cell_col = cells(cell, band_rows)
    from_col = cell_col + col_shift
    from_col = jnp.where(from_col >= GRID_W, from_col - GRID_W, from_col)
    skipped = band_rows - halo_rows
    source = jnp.where(cell < band_rows, (cell_row + row_shift) * GRID_W + from_col - skipped, -1)
    take_ref[...] = one_hot(source == lax.broadcasted_iota(jnp.int32, (rows, halo_rows), 1))
    take_own = one_hot(
        source - halo_rows == lax.broadcasted_iota(jnp.int32, (rows, band_rows), 1)
    )

    band = band_of(place[0], n_seq)

    def marks(index):
        row, col = cells(index, band_rows)
        wrap_row = (band * WIN + row >= GRID_H - row_shift).astype(jnp.int32)
        wrap_col = (col >= GRID_W - col_shift).astype(jnp.int32)
        return jnp.where(index < band_rows, (col // WIN) * 4 + 2 * wrap_row + wrap_col, -1)

    windows, queries, keys = same_ref.shape
    for w in range(windows):
        query = slab(w) + lax.broadcasted_iota(jnp.int32, (queries, 1), 0)
        key = slab(w) + lax.broadcasted_iota(jnp.int32, (1, keys), 1)
        same_ref[w] = (marks(query) == marks(key)).astype(jnp.int32)
    copies[1].wait()
    rolled_ref[...] = dot(take_own, own[...]).astype(jnp.bfloat16)
    for copy in copies[2:]:
        copy.wait()


def encode_kernel(
    blocks, place, rolled_ref, halo_ref, take_ref, same_ref, gain_ref, qkv_ref, out_ref, key_ref,
    value_ref, *sent
):
    rows = rolled_ref.shape[0]
    attn = HEADS * HEAD_DIM
    rolled = rolled_ref[...].astype(jnp.float32) + dot(take_ref[...], halo_ref[...])

    mean = jnp.mean(rolled, axis=-1, keepdims=True)
    centred = rolled - mean
    variance = jnp.mean(centred * centred, axis=-1, keepdims=True)
    normed = (centred * lax.rsqrt(variance + 1e-05) * gain_ref[...]).astype(jnp.bfloat16)
    qkv = dot(normed, qkv_ref[...])

    windows, queries, keys = same_ref.shape
    width = GROUP * HEAD_DIM
    lane_head = lax.broadcasted_iota(jnp.int32, (1, width), 1) // HEAD_DIM
    units = [(w, g) for w in range(windows) for g in range(HEADS // GROUP)]

    def taken(w, g, kind, count):
        at = kind * attn + g * width
        return qkv[slab(w) : slab(w) + count, at : at + width].astype(jnp.bfloat16)

    scores = []
    for w, g in units:
        q, k = taken(w, g, 0, queries), taken(w, g, 1, keys)
        stacked = jnp.concatenate(
            [jnp.where(lane_head == h, q, jnp.zeros_like(q)) for h in range(GROUP)], axis=0
        )
        scores.append(
            lax.dot_general(
                stacked, k, (((1,), (1,)), ((), ())), preferred_element_type=jnp.float32
            )
        )
    weights = []
    for (w, _), score in zip(units, scores):
        same = jnp.concatenate([same_ref[w]] * GROUP, axis=0) != 0
        score = jnp.where(same, score * HEAD_DIM ** (-0.5), -1000000000.0)
        score = jnp.exp(score - jnp.max(score, axis=-1, keepdims=True))
        total = jnp.sum(score, axis=-1, keepdims=True)
        weights.append((score * (1.0 / total)).astype(jnp.bfloat16))
    parts = [[] for _ in range(HEADS // GROUP)]
    for (w, g), weight in zip(units, weights):
        mixed = dot(weight, taken(w, g, 2, keys))
        mine = mixed[:queries]
        for h in range(1, GROUP):
            mine = jnp.where(lane_head == h, mixed[h * queries : (h + 1) * queries], mine)
        part = parts[g]
        if w == 0:
            part.append(mine)
            continue
        overlap = slab(w - 1) + queries - slab(w)
        row = slab(w) + lax.broadcasted_iota(jnp.int32, (overlap, 1), 0)
        last = part.pop()
        part.append(last[:-overlap])
        part.append(jnp.where(row < w * WIN * WIN, last[-overlap:], mine[:overlap]))
        part.append(mine[overlap:])
    pad = rows - slab(windows - 1) - queries
    parts = [
        jnp.concatenate([*part, jnp.zeros((pad, width), jnp.float32)], axis=0).astype(jnp.bfloat16)
        for part in parts
    ]
    attended = jnp.concatenate(parts, axis=1)
    memory = (rolled + dot(attended, out_ref[...])).astype(jnp.bfloat16)
    own_cols = sent[0].shape[1]
    for (is_value, r), block_ref in zip(blocks, sent):
        at = target(place, r, key_ref.shape[1] // own_cols) * own_cols
        weight_ref = value_ref if is_value else key_ref
        block = dot(memory, weight_ref[:, pl.ds(pl.multiple_of(at, own_cols), own_cols)])
        block_ref[...] = block[: block_ref.shape[0]].astype(jnp.bfloat16)


def select_kernel(n_seq, first, picks_ref, *refs):
    held, outs = refs[:n_seq], refs[n_seq:]
    for i, out in enumerate(outs):
        terms = [dot(picks_ref[first + i, r], held[r][...]) for r in range(n_seq)]
        out[...] = sum(terms[1:], terms[0]).astype(jnp.bfloat16)


def call(kernel, out_shape, n_scalar, n_vmem, flops, moved, n_hbm=0, scratch=()):
    return pl.pallas_call(
        kernel,
        out_shape=out_shape,
        in_specs=[SMEM] * n_scalar + [VMEM] * n_vmem + [HBM] * n_hbm,
        out_specs=jax.tree.map(lambda _: VMEM, out_shape),
        scratch_shapes=list(scratch),
        compiler_params=pltpu.CompilerParams(vmem_limit_bytes=VMEM_LIMIT),
        cost_estimate=pl.CostEstimate(flops=flops, bytes_accessed=moved, transcendentals=0),
    )


def local(
    memory_in, norm_gain, qkv_weight, out_weight, key_weight, value_weight, shift_offsets, row_order
):
    _, band_rows, emb = memory_in.shape
    n_seq = lax.axis_size("seq")
    n_tensor = lax.axis_size("tensor")
    own_cols = key_weight.shape[1] // n_seq
    pos = row_order.shape[1] // n_tensor
    rows = -(-band_rows // 16) * 16
    place = jnp.stack([lax.axis_index(axis) for axis in ("seq", "tensor", "dp")]).astype(jnp.int32)
    halo = rotated(memory_in[0, GRID_W :], "seq", 1)
    order = lax.dynamic_index_in_dim(row_order, lax.axis_index("tensor"), 0, False)
    order = order.reshape(n_tensor, pos, 1)

    weights = [qkv_weight, out_weight, key_weight, value_weight]
    off_chip = [shift_offsets, memory_in, norm_gain.reshape(1, emb), *weights]
    rolled_own, take, same, picks, gain, qkv_chip, out_chip, key_chip, value_chip = call(
        stage_kernel,
        [
            jax.ShapeDtypeStruct((rows, emb), jnp.bfloat16),
            jax.ShapeDtypeStruct((rows, halo.shape[0]), jnp.bfloat16),
            jax.ShapeDtypeStruct((GRID_W // WIN, *SLAB), jnp.int32),
            jax.ShapeDtypeStruct((n_tensor, n_seq, pos, band_rows), jnp.bfloat16),
            jax.ShapeDtypeStruct((1, emb), jnp.float32),
        ]
        + [jax.ShapeDtypeStruct(w.shape, w.dtype) for w in weights],
        1, 1, 50_000_000, 8_000_000, len(off_chip),
        [
            pltpu.SMEM(shift_offsets.shape, jnp.int32),
            pltpu.VMEM((band_rows, emb), jnp.bfloat16),
            pltpu.SemaphoreType.DMA((len(off_chip),)),
        ],
    )(place, order, *(pltpu.with_memory_space_constraint(x, pltpu.HBM) for x in off_chip))

    block = jax.ShapeDtypeStruct((band_rows, own_cols), jnp.bfloat16)
    blocks = [(is_value, r) for is_value in (False, True) for r in range(n_seq)]
    sent = call(
        functools.partial(encode_kernel, blocks), [block] * len(blocks),
        1, 9, 2_000_000_000, 10_000_000,
    )(place, rolled_own, halo, take, same, gain, qkv_chip, out_chip, key_chip, value_chip)
    held = [exchanged(b, r) if r else b for (_, r), b in zip(blocks, sent)]

    def selected(group, first, count):
        return call(
            functools.partial(select_kernel, n_seq, first),
            [jax.ShapeDtypeStruct((pos, own_cols), jnp.bfloat16)] * count,
            0, 1 + n_seq, 300_000_000, 1_000_000,
        )(picks, *held[group * n_seq : (group + 1) * n_seq])

    def gathered(group):
        away = selected(group, 1, n_tensor - 1)
        arrived = [rotated(away[d - 1], "tensor", d) for d in range(1, n_tensor)]
        return [*selected(group, 0, 1), *arrived]

    def by_page(blocks):
        page = jnp.arange(n_tensor)[:, None, None]
        result = blocks[0][None]
        for d in range(1, n_tensor):
            came = page == (lax.axis_index("tensor") - d) % n_tensor
            result = jnp.where(came, blocks[d][None], result)
        return jnp.broadcast_to(result, (n_tensor, pos, own_cols))

    key_out, value_blocks = lax.optimization_barrier((by_page(gathered(0)), gathered(1)))
    return key_out, by_page(value_blocks)


def solution(mesh):
    placed = (
        P(("dp", "tensor"), "seq", None),
        P(),
        P(),
        P(),
        P(),
        P(),
        P(("dp", "tensor"), None),
        P("dp", None),
    )
    return jax.shard_map(
        local,
        mesh=mesh,
        in_specs=placed,
        out_specs=(P("dp", "tensor", "seq"), P("dp", "tensor", "seq")),
        check_vma=False,
    )
```

```python
import functools

import jax
import jax.numpy as jnp
from jax import lax
from jax.experimental import pallas as pl
from jax.experimental.pallas import tpu as pltpu
from jax.sharding import PartitionSpec as P

HEADS = 16
HEAD_DIM = 32
GRID_H = 28
GRID_W = 21
WIN = 7

GROUP = 8
SLAB = (56, 64)
VMEM_LIMIT = 24 * 1024 * 1024

SMEM = pl.BlockSpec(memory_space=pltpu.SMEM)
VMEM = pl.BlockSpec(memory_space=pltpu.VMEM)
HBM = pl.BlockSpec(memory_space=pltpu.HBM)


def rotated(block, axis, distance):
    devices = lax.axis_size(axis)
    return lax.ppermute(block, axis, [(i, (i + distance) % devices) for i in range(devices)])


def paired(n):
    return n & (n - 1) == 0


def rounds_of(n):
    even = [*range(1, n)]
    odd = [*even[1:2], *even[:1], *even[2:]]
    return [(0, 0), *zip(even, odd)]


def distance(place, r, n):
    even, odd = rounds_of(n)[r]
    return jnp.where(lax.rem(place[2], 2) == 0, even, odd)


def target(place, r, n):
    d = distance(place, r, n)
    return place[0] ^ d if paired(n) else lax.rem(place[0] + d, n)


def origin(place, r, n):
    d = distance(place, r, n)
    return place[0] ^ d if paired(n) else lax.rem(place[0] - d + n, n)


def exchanged(block, r):
    n = lax.axis_size("seq")
    pairs = []
    for i in range(lax.axis_size("dp")):
        d = rounds_of(n)[r][i % 2]
        pairs += [(i * n + j, i * n + (j ^ d if paired(n) else (j + d) % n)) for j in range(n)]
    return lax.ppermute(block, ("dp", "seq"), pairs)


def band_of(seq, n_seq):
    return lax.rem(seq + n_seq - 1, n_seq)


def dot(a, b):
    return jnp.dot(a, b, preferred_element_type=jnp.float32)


def one_hot(cond):
    return jnp.where(cond, 1.0, 0.0).astype(jnp.bfloat16)


def cells(index, band_rows):
    window = index // (WIN * WIN)
    inside = index - window * (WIN * WIN)
    row = inside // WIN
    return row, window * WIN + inside - row * WIN


def slab(window):
    return window * WIN * WIN // 8 * 8


def stage_kernel(place, order_ref, shifts_hbm, pages_hbm, gain_hbm, *refs):
    weights, refs = refs[:4], refs[4:]
    rolled_ref, take_ref, same_ref, picks_ref, gain_ref, *staged = refs[:9]
    shifts, own, arrived = refs[9:]
    pairs = [(shifts_hbm, shifts), (pages_hbm.at[0], own), (gain_hbm, gain_ref)]
    pairs += list(zip(weights, staged))
    copies = [pltpu.make_async_copy(*pair, arrived.at[i]) for i, pair in enumerate(pairs)]
    for copy in copies:
        copy.start()
    band_rows = own.shape[0]
    rows, halo_rows = take_ref.shape
    n_tensor, n_seq, pos, _ = picks_ref.shape
    for i in range(n_tensor):
        order = order_ref[lax.rem(place[1] + i, n_tensor)]
        order_band = order // band_rows
        row = (order - order_band * band_rows) // GRID_W
        col = order - order_band * band_rows - row * GRID_W
        window = col // WIN
        cell_at = (window * WIN + row) * WIN + col - window * WIN
        for r in range(n_seq):
            band = band_of(origin(place, r, n_seq), n_seq)
            at = jnp.where(order_band == band, cell_at, -1)
            picks_ref[i, r] = one_hot(at == lax.broadcasted_iota(jnp.int32, (1, band_rows), 1))
    copies[0].wait()
    row_shift, col_shift = shifts[0, 0], shifts[0, 1]

    cell = lax.broadcasted_iota(jnp.int32, (rows, 1), 0)
    cell_row, cell_col = cells(cell, band_rows)
    from_col = cell_col + col_shift
    from_col = jnp.where(from_col >= GRID_W, from_col - GRID_W, from_col)
    skipped = band_rows - halo_rows
    source = jnp.where(cell < band_rows, (cell_row + row_shift) * GRID_W + from_col - skipped, -1)
    take_ref[...] = one_hot(source == lax.broadcasted_iota(jnp.int32, (rows, halo_rows), 1))
    take_own = one_hot(
        source - halo_rows == lax.broadcasted_iota(jnp.int32, (rows, band_rows), 1)
    )

    band = band_of(place[0], n_seq)

    def marks(index):
        row, col = cells(index, band_rows)
        wrap_row = (band * WIN + row >= GRID_H - row_shift).astype(jnp.int32)
        wrap_col = (col >= GRID_W - col_shift).astype(jnp.int32)
        return jnp.where(index < band_rows, (col // WIN) * 4 + 2 * wrap_row + wrap_col, -1)

    windows, queries, keys = same_ref.shape
    for w in range(windows):
        query = slab(w) + lax.broadcasted_iota(jnp.int32, (queries, 1), 0)
        key = slab(w) + lax.broadcasted_iota(jnp.int32, (1, keys), 1)
        same_ref[w] = (marks(query) == marks(key)).astype(jnp.int32)
    copies[1].wait()
    rolled_ref[...] = dot(take_own, own[...]).astype(jnp.bfloat16)
    for copy in copies[2:]:
        copy.wait()


def encode_kernel(
    blocks, place, rolled_ref, halo_ref, take_ref, same_ref, gain_ref, qkv_ref, out_ref, key_ref,
    value_ref, *sent
):
    rows = rolled_ref.shape[0]
    attn = HEADS * HEAD_DIM
    rolled = rolled_ref[...].astype(jnp.float32) + dot(take_ref[...], halo_ref[...])

    mean = jnp.mean(rolled, axis=-1, keepdims=True)
    centred = rolled - mean
    variance = jnp.mean(centred * centred, axis=-1, keepdims=True)
    normed = (centred * lax.rsqrt(variance + 1e-05) * gain_ref[...]).astype(jnp.bfloat16)
    qkv = dot(normed, qkv_ref[...])

    windows, queries, keys = same_ref.shape
    width = GROUP * HEAD_DIM
    lane_head = lax.broadcasted_iota(jnp.int32, (1, width), 1) // HEAD_DIM
    units = [(w, g) for w in range(windows) for g in range(HEADS // GROUP)]

    def taken(w, g, kind, count):
        at = kind * attn + g * width
        return qkv[slab(w) : slab(w) + count, at : at + width].astype(jnp.bfloat16)

    scores = []
    for w, g in units:
        q, k = taken(w, g, 0, queries), taken(w, g, 1, keys)
        stacked = jnp.concatenate(
            [jnp.where(lane_head == h, q, jnp.zeros_like(q)) for h in range(GROUP)], axis=0
        )
        scores.append(
            lax.dot_general(
                stacked, k, (((1,), (1,)), ((), ())), preferred_element_type=jnp.float32
            )
        )
    weights = []
    for (w, _), score in zip(units, scores):
        same = jnp.concatenate([same_ref[w]] * GROUP, axis=0) != 0
        score = jnp.where(same, score * HEAD_DIM ** (-0.5), -1000000000.0)
        score = jnp.exp(score - jnp.max(score, axis=-1, keepdims=True))
        total = jnp.sum(score, axis=-1, keepdims=True)
        weights.append((score * (1.0 / total)).astype(jnp.bfloat16))
    parts = [[] for _ in range(HEADS // GROUP)]
    for (w, g), weight in zip(units, weights):
        mixed = dot(weight, taken(w, g, 2, keys))
        mine = mixed[:queries]
        for h in range(1, GROUP):
            mine = jnp.where(lane_head == h, mixed[h * queries : (h + 1) * queries], mine)
        part = parts[g]
        if w == 0:
            part.append(mine)
            continue
        overlap = slab(w - 1) + queries - slab(w)
        row = slab(w) + lax.broadcasted_iota(jnp.int32, (overlap, 1), 0)
        last = part.pop()
        part.append(last[:-overlap])
        part.append(jnp.where(row < w * WIN * WIN, last[-overlap:], mine[:overlap]))
        part.append(mine[overlap:])
    pad = rows - slab(windows - 1) - queries
    parts = [
        jnp.concatenate([*part, jnp.zeros((pad, width), jnp.float32)], axis=0).astype(jnp.bfloat16)
        for part in parts
    ]
    attended = jnp.concatenate(parts, axis=1)
    memory = (rolled + dot(attended, out_ref[...])).astype(jnp.bfloat16)
    n_seq = 1 + max(r for _, r in blocks)
    own_cols = key_ref.shape[1] // n_seq
    for (kinds, r), block_ref in zip(blocks, sent):
        at = pl.multiple_of(target(place, r, n_seq) * own_cols, own_cols)
        for i, kind in enumerate(kinds):
            block = dot(memory, (key_ref, value_ref)[kind][:, pl.ds(at, own_cols)])
            cols = slice(i * own_cols, (i + 1) * own_cols)
            block_ref[:, cols] = block[: block_ref.shape[0]].astype(jnp.bfloat16)


def select_kernel(rounds, first, picks_ref, *refs):
    held, outs = refs[: len(rounds)], refs[len(rounds) :]
    for i, out in enumerate(outs):
        width = out.shape[1]
        terms = [
            dot(picks_ref[first + i, r], ref[:, at * width : (at + 1) * width])
            for (r, at), ref in zip(rounds, held)
        ]
        out[...] = sum(terms[1:], terms[0]).astype(jnp.bfloat16)


def call(kernel, out_shape, n_scalar, n_vmem, flops, moved, n_hbm=0, scratch=()):
    return pl.pallas_call(
        kernel,
        out_shape=out_shape,
        in_specs=[SMEM] * n_scalar + [VMEM] * n_vmem + [HBM] * n_hbm,
        out_specs=jax.tree.map(lambda _: VMEM, out_shape),
        scratch_shapes=list(scratch),
        compiler_params=pltpu.CompilerParams(vmem_limit_bytes=VMEM_LIMIT),
        cost_estimate=pl.CostEstimate(flops=flops, bytes_accessed=moved, transcendentals=0),
    )


def local(
    memory_in, norm_gain, qkv_weight, out_weight, key_weight, value_weight, shift_offsets, row_order
):
    _, band_rows, emb = memory_in.shape
    n_seq = lax.axis_size("seq")
    n_tensor = lax.axis_size("tensor")
    own_cols = key_weight.shape[1] // n_seq
    pos = row_order.shape[1] // n_tensor
    rows = -(-band_rows // 16) * 16
    place = jnp.stack([lax.axis_index(axis) for axis in ("seq", "tensor", "dp")]).astype(jnp.int32)
    halo = rotated(memory_in[0, GRID_W :], "seq", 1)
    order = lax.dynamic_index_in_dim(row_order, lax.axis_index("tensor"), 0, False)
    order = order.reshape(n_tensor, pos, 1)

    weights = [qkv_weight, out_weight, key_weight, value_weight]
    off_chip = [shift_offsets, memory_in, norm_gain.reshape(1, emb), *weights]
    rolled_own, take, same, picks, gain, qkv_chip, out_chip, key_chip, value_chip = call(
        stage_kernel,
        [
            jax.ShapeDtypeStruct((rows, emb), jnp.bfloat16),
            jax.ShapeDtypeStruct((rows, halo.shape[0]), jnp.bfloat16),
            jax.ShapeDtypeStruct((GRID_W // WIN, *SLAB), jnp.int32),
            jax.ShapeDtypeStruct((n_tensor, n_seq, pos, band_rows), jnp.bfloat16),
            jax.ShapeDtypeStruct((1, emb), jnp.float32),
        ]
        + [jax.ShapeDtypeStruct(w.shape, w.dtype) for w in weights],
        1, 1, 50_000_000, 8_000_000, len(off_chip),
        [
            pltpu.SMEM(shift_offsets.shape, jnp.int32),
            pltpu.VMEM((band_rows, emb), jnp.bfloat16),
            pltpu.SemaphoreType.DMA((len(off_chip),)),
        ],
    )(place, order, *(pltpu.with_memory_space_constraint(x, pltpu.HBM) for x in off_chip))

    apart = [0, *range(2, n_seq)]
    blocks = [((0,), r) for r in apart] + [((0, 1), 1)] + [((1,), r) for r in apart]
    sent = call(
        functools.partial(encode_kernel, blocks),
        [
            jax.ShapeDtypeStruct((band_rows, len(kinds) * own_cols), jnp.bfloat16)
            for kinds, _ in blocks
        ],
        1, 9, 2_000_000_000, 10_000_000,
    )(place, rolled_own, halo, take, same, gain, qkv_chip, out_chip, key_chip, value_chip)
    held = [exchanged(b, r) if r else b for (_, r), b in zip(blocks, sent)]

    def selected(kind, first, count):
        mine = [(r, kinds.index(kind), b) for (kinds, r), b in zip(blocks, held) if kind in kinds]
        return call(
            functools.partial(select_kernel, [(r, at) for r, at, _ in mine], first),
            [jax.ShapeDtypeStruct((pos, own_cols), jnp.bfloat16)] * count,
            0, 1 + n_seq, 300_000_000, 1_000_000,
        )(picks, *(b for *_, b in mine))

    def gathered(group):
        away = selected(group, 1, n_tensor - 1)
        arrived = [rotated(away[d - 1], "tensor", d) for d in range(1, n_tensor)]
        return [*selected(group, 0, 1), *arrived]

    def by_page(blocks):
        page = jnp.arange(n_tensor)[:, None, None]
        result = blocks[0][None]
        for d in range(1, n_tensor):
            came = page == (lax.axis_index("tensor") - d) % n_tensor
            result = jnp.where(came, blocks[d][None], result)
        return jnp.broadcast_to(result, (n_tensor, pos, own_cols))

    key_out, value_blocks = lax.optimization_barrier((by_page(gathered(0)), gathered(1)))
    return key_out, by_page(value_blocks)


def solution(mesh):
    placed = (
        P(("dp", "tensor"), "seq", None),
        P(),
        P(),
        P(),
        P(),
        P(),
        P(("dp", "tensor"), None),
        P("dp", None),
    )
    return jax.shard_map(
        local,
        mesh=mesh,
        in_specs=placed,
        out_specs=(P("dp", "tensor", "seq"), P("dp", "tensor", "seq")),
        check_vma=False,
    )
```

```python
import functools

import jax
import jax.numpy as jnp
from jax import lax
from jax.experimental import pallas as pl
from jax.experimental.pallas import tpu as pltpu
from jax.sharding import PartitionSpec as P

HEADS = 16
HEAD_DIM = 32
GRID_H = 28
GRID_W = 21
WIN = 7

GROUP = 8
SLAB = (56, 64)
VMEM_LIMIT = 24 * 1024 * 1024

SMEM = pl.BlockSpec(memory_space=pltpu.SMEM)
VMEM = pl.BlockSpec(memory_space=pltpu.VMEM)
HBM = pl.BlockSpec(memory_space=pltpu.HBM)


def rotated(block, axis, distance):
    devices = lax.axis_size(axis)
    return lax.ppermute(block, axis, [(i, (i + distance) % devices) for i in range(devices)])


def paired(n):
    return n & (n - 1) == 0


def rounds_of(n):
    even = [*range(1, n)]
    odd = [*even[1:2], *even[:1], *even[2:]]
    return [(0, 0), *zip(even, odd)]


def distance(place, r, n):
    even, odd = rounds_of(n)[r]
    return jnp.where(lax.rem(place[2], 2) == 0, even, odd)


def target(place, r, n):
    d = distance(place, r, n)
    return place[0] ^ d if paired(n) else lax.rem(place[0] + d, n)


def origin(place, r, n):
    d = distance(place, r, n)
    return place[0] ^ d if paired(n) else lax.rem(place[0] - d + n, n)


def exchanged(block, r):
    n = lax.axis_size("seq")
    pairs = []
    for i in range(lax.axis_size("dp")):
        d = rounds_of(n)[r][i % 2]
        pairs += [(i * n + j, i * n + (j ^ d if paired(n) else (j + d) % n)) for j in range(n)]
    return lax.ppermute(block, ("dp", "seq"), pairs)


def band_of(seq, n_seq):
    return lax.rem(seq + n_seq - 1, n_seq)


def dot(a, b):
    return jnp.dot(a, b, preferred_element_type=jnp.float32)


def one_hot(cond):
    return jnp.where(cond, 1.0, 0.0).astype(jnp.bfloat16)


def cells(index, band_rows):
    window = index // (WIN * WIN)
    inside = index - window * (WIN * WIN)
    row = inside // WIN
    return row, window * WIN + inside - row * WIN


def slab(window):
    return window * WIN * WIN // 8 * 8


def stage_kernel(place, order_ref, shifts_hbm, pages_hbm, gain_hbm, *refs):
    weights, refs = refs[:4], refs[4:]
    rolled_ref, take_ref, same_ref, picks_ref, gain_ref, *staged = refs[:9]
    shifts, own, arrived = refs[9:]
    pairs = [(shifts_hbm, shifts), (pages_hbm.at[0], own), (gain_hbm, gain_ref)]
    pairs += list(zip(weights, staged))
    copies = [pltpu.make_async_copy(*pair, arrived.at[i]) for i, pair in enumerate(pairs)]
    for copy in copies:
        copy.start()
    band_rows = own.shape[0]
    rows, halo_rows = take_ref.shape
    n_tensor, n_seq, pos, _ = picks_ref.shape
    for i in range(n_tensor):
        order = order_ref[lax.rem(place[1] + i, n_tensor)]
        order_band = order // band_rows
        row = (order - order_band * band_rows) // GRID_W
        col = order - order_band * band_rows - row * GRID_W
        window = col // WIN
        cell_at = (window * WIN + row) * WIN + col - window * WIN
        for r in range(n_seq):
            band = band_of(origin(place, r, n_seq), n_seq)
            at = jnp.where(order_band == band, cell_at, -1)
            picks_ref[i, r] = one_hot(at == lax.broadcasted_iota(jnp.int32, (1, band_rows), 1))
    copies[0].wait()
    row_shift, col_shift = shifts[0, 0], shifts[0, 1]

    cell = lax.broadcasted_iota(jnp.int32, (rows, 1), 0)
    cell_row, cell_col = cells(cell, band_rows)
    from_col = cell_col + col_shift
    from_col = jnp.where(from_col >= GRID_W, from_col - GRID_W, from_col)
    skipped = band_rows - halo_rows
    source = jnp.where(cell < band_rows, (cell_row + row_shift) * GRID_W + from_col - skipped, -1)
    take_ref[...] = one_hot(source == lax.broadcasted_iota(jnp.int32, (rows, halo_rows), 1))
    take_own = one_hot(
        source - halo_rows == lax.broadcasted_iota(jnp.int32, (rows, band_rows), 1)
    )

    band = band_of(place[0], n_seq)

    def marks(index):
        row, col = cells(index, band_rows)
        wrap_row = (band * WIN + row >= GRID_H - row_shift).astype(jnp.int32)
        wrap_col = (col >= GRID_W - col_shift).astype(jnp.int32)
        return jnp.where(index < band_rows, (col // WIN) * 4 + 2 * wrap_row + wrap_col, -1)

    windows, queries, keys = same_ref.shape
    for w in range(windows):
        query = slab(w) + lax.broadcasted_iota(jnp.int32, (queries, 1), 0)
        key = slab(w) + lax.broadcasted_iota(jnp.int32, (1, keys), 1)
        same_ref[w] = (marks(query) == marks(key)).astype(jnp.int32)
    copies[1].wait()
    rolled_ref[...] = dot(take_own, own[...]).astype(jnp.bfloat16)
    for copy in copies[2:]:
        copy.wait()


def encode_kernel(
    blocks, band_rows, place, rolled_ref, halo_ref, take_ref, same_ref, gain_ref, qkv_ref, out_ref, key_ref,
    value_ref, *sent
):
    rows = rolled_ref.shape[0]
    attn = HEADS * HEAD_DIM
    rolled = rolled_ref[...].astype(jnp.float32) + dot(take_ref[...], halo_ref[...])

    mean = jnp.mean(rolled, axis=-1, keepdims=True)
    centred = rolled - mean
    variance = jnp.mean(centred * centred, axis=-1, keepdims=True)
    normed = (centred * lax.rsqrt(variance + 1e-05) * gain_ref[...]).astype(jnp.bfloat16)
    qkv = dot(normed, qkv_ref[...])

    windows, queries, keys = same_ref.shape
    width = GROUP * HEAD_DIM
    lane_head = lax.broadcasted_iota(jnp.int32, (1, width), 1) // HEAD_DIM
    units = [(w, g) for w in range(windows) for g in range(HEADS // GROUP)]

    def taken(w, g, kind, count):
        at = kind * attn + g * width
        return qkv[slab(w) : slab(w) + count, at : at + width].astype(jnp.bfloat16)

    scores = []
    for w, g in units:
        q, k = taken(w, g, 0, queries), taken(w, g, 1, keys)
        stacked = jnp.concatenate(
            [jnp.where(lane_head == h, q, jnp.zeros_like(q)) for h in range(GROUP)], axis=0
        )
        scores.append(
            lax.dot_general(
                stacked, k, (((1,), (1,)), ((), ())), preferred_element_type=jnp.float32
            )
        )
    weights = []
    for (w, _), score in zip(units, scores):
        same = jnp.concatenate([same_ref[w]] * GROUP, axis=0) != 0
        score = jnp.where(same, score * HEAD_DIM ** (-0.5), -1000000000.0)
        score = jnp.exp(score - jnp.max(score, axis=-1, keepdims=True))
        total = jnp.sum(score, axis=-1, keepdims=True)
        weights.append((score * (1.0 / total)).astype(jnp.bfloat16))
    parts = [[] for _ in range(HEADS // GROUP)]
    for (w, g), weight in zip(units, weights):
        mixed = dot(weight, taken(w, g, 2, keys))
        mine = mixed[:queries]
        for h in range(1, GROUP):
            mine = jnp.where(lane_head == h, mixed[h * queries : (h + 1) * queries], mine)
        part = parts[g]
        if w == 0:
            part.append(mine)
            continue
        overlap = slab(w - 1) + queries - slab(w)
        row = slab(w) + lax.broadcasted_iota(jnp.int32, (overlap, 1), 0)
        last = part.pop()
        part.append(last[:-overlap])
        part.append(jnp.where(row < w * WIN * WIN, last[-overlap:], mine[:overlap]))
        part.append(mine[overlap:])
    pad = rows - slab(windows - 1) - queries
    parts = [
        jnp.concatenate([*part, jnp.zeros((pad, width), jnp.float32)], axis=0).astype(jnp.bfloat16)
        for part in parts
    ]
    attended = jnp.concatenate(parts, axis=1)
    memory = (rolled + dot(attended, out_ref[...])).astype(jnp.bfloat16)
    n_seq = 1 + max(r for _, r in blocks)
    own_cols = key_ref.shape[1] // n_seq

    def block(kind, r):
        at = pl.multiple_of(target(place, r, n_seq) * own_cols, own_cols)
        return dot(memory, (key_ref, value_ref)[kind][:, pl.ds(at, own_cols)])

    apart = {r for kinds, r in blocks if kinds == (0,)}
    values = {r: block(1, r) for r in apart}
    for (kinds, r), block_ref in zip(blocks, sent):
        count = block_ref.shape[0]
        if kinds == (1,):
            block_ref[...] = values[r][:count].astype(jnp.bfloat16)
        elif kinds == (0,):
            keys = block(0, r)
            whole = count // 8 * 8
            extra = count - band_rows
            spot = lax.broadcasted_iota(jnp.int32, (8, 1), 0)
            moved = pltpu.roll(values[r][whole : whole + 8], extra, 0)
            tail = jnp.where(spot < band_rows - whole, keys[whole : whole + 8], moved)
            both = jnp.concatenate([keys[:whole], tail], axis=0)
            block_ref[...] = both[:count].astype(jnp.bfloat16)
        else:
            for i, kind in enumerate(kinds):
                cols = slice(i * own_cols, (i + 1) * own_cols)
                block_ref[:, cols] = block(kind, r)[:count].astype(jnp.bfloat16)


def select_kernel(rounds, first, picks_ref, *refs):
    outs = refs[sum(1 + rest for *_, rest in rounds) :]
    refs = iter(refs)
    band_rows = picks_ref.shape[-1]
    width = outs[0].shape[1]
    blocks = []
    for r, at, rest in rounds:
        block = next(refs)[:, at * width : (at + 1) * width]
        if rest:
            whole = block.shape[0]
            last = next(refs)[whole:, :].astype(jnp.float32)
            last = last[band_rows - whole :].astype(jnp.bfloat16)
            block = jnp.concatenate([block, last], axis=0)
        blocks.append((r, block[:band_rows]))
    for i, out in enumerate(outs):
        terms = [dot(picks_ref[first + i, r], block) for r, block in blocks]
        out[...] = sum(terms[1:], terms[0]).astype(jnp.bfloat16)


def call(kernel, out_shape, n_scalar, n_vmem, flops, moved, n_hbm=0, scratch=()):
    return pl.pallas_call(
        kernel,
        out_shape=out_shape,
        in_specs=[SMEM] * n_scalar + [VMEM] * n_vmem + [HBM] * n_hbm,
        out_specs=jax.tree.map(lambda _: VMEM, out_shape),
        scratch_shapes=list(scratch),
        compiler_params=pltpu.CompilerParams(vmem_limit_bytes=VMEM_LIMIT),
        cost_estimate=pl.CostEstimate(flops=flops, bytes_accessed=moved, transcendentals=0),
    )


def local(
    memory_in, norm_gain, qkv_weight, out_weight, key_weight, value_weight, shift_offsets, row_order
):
    _, band_rows, emb = memory_in.shape
    n_seq = lax.axis_size("seq")
    n_tensor = lax.axis_size("tensor")
    own_cols = key_weight.shape[1] // n_seq
    pos = row_order.shape[1] // n_tensor
    rows = -(-band_rows // 16) * 16
    place = jnp.stack([lax.axis_index(axis) for axis in ("seq", "tensor", "dp")]).astype(jnp.int32)
    halo = rotated(memory_in[0, GRID_W :], "seq", 1)
    order = lax.dynamic_index_in_dim(row_order, lax.axis_index("tensor"), 0, False)
    order = order.reshape(n_tensor, pos, 1)

    weights = [qkv_weight, out_weight, key_weight, value_weight]
    off_chip = [shift_offsets, memory_in, norm_gain.reshape(1, emb), *weights]
    rolled_own, take, same, picks, gain, qkv_chip, out_chip, key_chip, value_chip = call(
        stage_kernel,
        [
            jax.ShapeDtypeStruct((rows, emb), jnp.bfloat16),
            jax.ShapeDtypeStruct((rows, halo.shape[0]), jnp.bfloat16),
            jax.ShapeDtypeStruct((GRID_W // WIN, *SLAB), jnp.int32),
            jax.ShapeDtypeStruct((n_tensor, n_seq, pos, band_rows), jnp.bfloat16),
            jax.ShapeDtypeStruct((1, emb), jnp.float32),
        ]
        + [jax.ShapeDtypeStruct(w.shape, w.dtype) for w in weights],
        1, 1, 50_000_000, 8_000_000, len(off_chip),
        [
            pltpu.SMEM(shift_offsets.shape, jnp.int32),
            pltpu.VMEM((band_rows, emb), jnp.bfloat16),
            pltpu.SemaphoreType.DMA((len(off_chip),)),
        ],
    )(place, order, *(pltpu.with_memory_space_constraint(x, pltpu.HBM) for x in off_chip))

    apart = [0, *range(2, n_seq)]
    blocks = [((0,), r) for r in apart] + [((0, 1), 1)] + [((1,), r) for r in apart]
    whole = band_rows // 16 * 16
    counts = {(0,): 2 * band_rows - whole, (0, 1): band_rows, (1,): whole}
    sent = call(
        functools.partial(encode_kernel, blocks, band_rows),
        [
            jax.ShapeDtypeStruct((counts[kinds], len(kinds) * own_cols), jnp.bfloat16)
            for kinds, _ in blocks
        ],
        1, 9, 2_000_000_000, 10_000_000,
    )(place, rolled_own, halo, take, same, gain, qkv_chip, out_chip, key_chip, value_chip)
    held = [exchanged(b, r) if r else b for (_, r), b in zip(blocks, sent)]

    def selected(kind, first, count):
        mine, operands = [], []
        for (kinds, r), b in zip(blocks, held):
            if kind in kinds:
                rest = kinds == (1,)
                mine.append((r, kinds.index(kind), int(rest)))
                operands += [b, held[blocks.index(((0,), r))]] if rest else [b]
        return call(
            functools.partial(select_kernel, mine, first),
            [jax.ShapeDtypeStruct((pos, own_cols), jnp.bfloat16)] * count,
            0, 1 + len(operands), 300_000_000, 1_000_000,
        )(picks, *operands)

    def gathered(group):
        away = selected(group, 1, n_tensor - 1)
        arrived = [rotated(away[d - 1], "tensor", d) for d in range(1, n_tensor)]
        return [*selected(group, 0, 1), *arrived]

    def by_page(blocks):
        page = jnp.arange(n_tensor)[:, None, None]
        result = blocks[0][None]
        for d in range(1, n_tensor):
            came = page == (lax.axis_index("tensor") - d) % n_tensor
            result = jnp.where(came, blocks[d][None], result)
        return jnp.broadcast_to(result, (n_tensor, pos, own_cols))

    key_out, value_blocks = lax.optimization_barrier((by_page(gathered(0)), gathered(1)))
    return key_out, by_page(value_blocks)


def solution(mesh):
    placed = (
        P(("dp", "tensor"), "seq", None),
        P(),
        P(),
        P(),
        P(),
        P(),
        P(("dp", "tensor"), None),
        P("dp", None),
    )
    return jax.shard_map(
        local,
        mesh=mesh,
        in_specs=placed,
        out_specs=(P("dp", "tensor", "seq"), P("dp", "tensor", "seq")),
        check_vma=False,
    )
```

```python
import functools

import jax
import jax.numpy as jnp
from jax import lax
from jax.experimental import pallas as pl
from jax.experimental.pallas import tpu as pltpu
from jax.sharding import PartitionSpec as P

HEADS = 16
HEAD_DIM = 32
GRID_H = 28
GRID_W = 21
WIN = 7

GROUP = 4
SLAB = (56, 64)
VMEM_LIMIT = 24 * 1024 * 1024

SMEM = pl.BlockSpec(memory_space=pltpu.SMEM)
VMEM = pl.BlockSpec(memory_space=pltpu.VMEM)
HBM = pl.BlockSpec(memory_space=pltpu.HBM)


def rotated(block, axis, distance):
    devices = lax.axis_size(axis)
    return lax.ppermute(block, axis, [(i, (i + distance) % devices) for i in range(devices)])


def paired(n):
    return n & (n - 1) == 0


def rounds_of(n):
    even = [*range(1, n)]
    odd = [*even[1:2], *even[:1], *even[2:]]
    return [(0, 0), *zip(even, odd)]


def distance(place, r, n):
    even, odd = rounds_of(n)[r]
    return jnp.where(lax.rem(place[2], 2) == 0, even, odd)


def target(place, r, n):
    d = distance(place, r, n)
    return place[0] ^ d if paired(n) else lax.rem(place[0] + d, n)


def origin(place, r, n):
    d = distance(place, r, n)
    return place[0] ^ d if paired(n) else lax.rem(place[0] - d + n, n)


def exchanged(block, r):
    n = lax.axis_size("seq")
    pairs = []
    for i in range(lax.axis_size("dp")):
        d = rounds_of(n)[r][i % 2]
        pairs += [(i * n + j, i * n + (j ^ d if paired(n) else (j + d) % n)) for j in range(n)]
    return lax.ppermute(block, ("dp", "seq"), pairs)


def band_of(seq, n_seq):
    return lax.rem(seq + n_seq - 1, n_seq)


def dot(a, b):
    return jnp.dot(a, b, preferred_element_type=jnp.float32)


def one_hot(cond):
    return jnp.where(cond, 1.0, 0.0).astype(jnp.bfloat16)


def cells(index, band_rows):
    window = index // (WIN * WIN)
    inside = index - window * (WIN * WIN)
    row = inside // WIN
    return row, window * WIN + inside - row * WIN


def slab(window):
    return window * WIN * WIN // 8 * 8


def stage_kernel(place, order_ref, shifts_hbm, pages_hbm, gain_hbm, *refs):
    weights, refs = refs[:4], refs[4:]
    rolled_ref, take_ref, same_ref, picks_ref, gain_ref, *staged = refs[:9]
    shifts, own, arrived = refs[9:]
    pairs = [(shifts_hbm, shifts), (pages_hbm.at[0], own), (gain_hbm, gain_ref)]
    pairs += list(zip(weights, staged))
    copies = [pltpu.make_async_copy(*pair, arrived.at[i]) for i, pair in enumerate(pairs)]
    for copy in copies:
        copy.start()
    band_rows = own.shape[0]
    rows, halo_rows = take_ref.shape
    n_tensor, n_seq, pos, _ = picks_ref.shape
    for i in range(n_tensor):
        order = order_ref[lax.rem(place[1] + i, n_tensor)]
        order_band = order // band_rows
        row = (order - order_band * band_rows) // GRID_W
        col = order - order_band * band_rows - row * GRID_W
        window = col // WIN
        cell_at = (window * WIN + row) * WIN + col - window * WIN
        for r in range(n_seq):
            band = band_of(origin(place, r, n_seq), n_seq)
            at = jnp.where(order_band == band, cell_at, -1)
            picks_ref[i, r] = one_hot(at == lax.broadcasted_iota(jnp.int32, (1, band_rows), 1))
    copies[0].wait()
    row_shift, col_shift = shifts[0, 0], shifts[0, 1]

    cell = lax.broadcasted_iota(jnp.int32, (rows, 1), 0)
    cell_row, cell_col = cells(cell, band_rows)
    from_col = cell_col + col_shift
    from_col = jnp.where(from_col >= GRID_W, from_col - GRID_W, from_col)
    skipped = band_rows - halo_rows
    source = jnp.where(cell < band_rows, (cell_row + row_shift) * GRID_W + from_col - skipped, -1)
    take_ref[...] = one_hot(source == lax.broadcasted_iota(jnp.int32, (rows, halo_rows), 1))
    take_own = one_hot(
        source - halo_rows == lax.broadcasted_iota(jnp.int32, (rows, band_rows), 1)
    )

    band = band_of(place[0], n_seq)

    def marks(index):
        row, col = cells(index, band_rows)
        wrap_row = (band * WIN + row >= GRID_H - row_shift).astype(jnp.int32)
        wrap_col = (col >= GRID_W - col_shift).astype(jnp.int32)
        return jnp.where(index < band_rows, (col // WIN) * 4 + 2 * wrap_row + wrap_col, -1)

    windows, queries, keys = same_ref.shape
    for w in range(windows):
        query = slab(w) + lax.broadcasted_iota(jnp.int32, (queries, 1), 0)
        key = slab(w) + lax.broadcasted_iota(jnp.int32, (1, keys), 1)
        same_ref[w] = (marks(query) == marks(key)).astype(jnp.int32)
    copies[1].wait()
    rolled_ref[...] = dot(take_own, own[...]).astype(jnp.bfloat16)
    for copy in copies[2:]:
        copy.wait()


def encode_kernel(
    blocks, band_rows, place, rolled_ref, halo_ref, take_ref, same_ref, gain_ref, qkv_ref, out_ref, key_ref,
    value_ref, *sent
):
    rows = rolled_ref.shape[0]
    attn = HEADS * HEAD_DIM
    rolled = rolled_ref[...].astype(jnp.float32) + dot(take_ref[...], halo_ref[...])

    mean = jnp.mean(rolled, axis=-1, keepdims=True)
    centred = rolled - mean
    variance = jnp.mean(centred * centred, axis=-1, keepdims=True)
    normed = (centred * lax.rsqrt(variance + 1e-05) * gain_ref[...]).astype(jnp.bfloat16)
    qkv = dot(normed, qkv_ref[...])

    windows, queries, keys = same_ref.shape
    width = GROUP * HEAD_DIM
    lane_head = lax.broadcasted_iota(jnp.int32, (1, width), 1) // HEAD_DIM
    units = [(w, g) for w in range(windows) for g in range(HEADS // GROUP)]

    def taken(w, g, kind, count):
        at = kind * attn + g * width
        return qkv[slab(w) : slab(w) + count, at : at + width].astype(jnp.bfloat16)

    scores = []
    for w, g in units:
        q, k = taken(w, g, 0, queries), taken(w, g, 1, keys)
        stacked = jnp.concatenate(
            [jnp.where(lane_head == h, q, jnp.zeros_like(q)) for h in range(GROUP)], axis=0
        )
        scores.append(
            lax.dot_general(
                stacked, k, (((1,), (1,)), ((), ())), preferred_element_type=jnp.float32
            )
        )
    weights = []
    for (w, _), score in zip(units, scores):
        same = jnp.concatenate([same_ref[w]] * GROUP, axis=0) != 0
        score = jnp.where(same, score * HEAD_DIM ** (-0.5), -1000000000.0)
        score = jnp.exp(score - jnp.max(score, axis=-1, keepdims=True))
        total = jnp.sum(score, axis=-1, keepdims=True)
        weights.append((score.astype(jnp.bfloat16), 1.0 / total))
    parts = [[] for _ in range(HEADS // GROUP)]
    for (w, g), weight in zip(units, weights):
        mixed = dot(weight[0], taken(w, g, 2, keys)) * weight[1]
        mine = mixed[:queries]
        for h in range(1, GROUP):
            mine = jnp.where(lane_head == h, mixed[h * queries : (h + 1) * queries], mine)
        part = parts[g]
        if w == 0:
            part.append(mine)
            continue
        overlap = slab(w - 1) + queries - slab(w)
        row = slab(w) + lax.broadcasted_iota(jnp.int32, (overlap, 1), 0)
        last = part.pop()
        part.append(last[:-overlap])
        part.append(jnp.where(row < w * WIN * WIN, last[-overlap:], mine[:overlap]))
        part.append(mine[overlap:])
    pad = rows - slab(windows - 1) - queries
    parts = [
        jnp.concatenate([*part, jnp.zeros((pad, width), jnp.float32)], axis=0).astype(jnp.bfloat16)
        for part in parts
    ]
    attended = jnp.concatenate(parts, axis=1)
    memory = (rolled + dot(attended, out_ref[...])).astype(jnp.bfloat16)
    n_seq = 1 + max(r for _, r in blocks)
    own_cols = key_ref.shape[1] // n_seq

    def block(kind, r):
        at = pl.multiple_of(target(place, r, n_seq) * own_cols, own_cols)
        return dot(memory, (key_ref, value_ref)[kind][:, pl.ds(at, own_cols)])

    apart = {r for kinds, r in blocks if kinds == (0,)}
    values = {r: block(1, r) for r in apart}
    for (kinds, r), block_ref in zip(blocks, sent):
        count = block_ref.shape[0]
        if kinds == (1,):
            block_ref[...] = values[r][:count].astype(jnp.bfloat16)
        elif kinds == (0,):
            keys = block(0, r)
            whole = count // 8 * 8
            extra = count - band_rows
            spot = lax.broadcasted_iota(jnp.int32, (8, 1), 0)
            moved = pltpu.roll(values[r][whole : whole + 8], extra, 0)
            tail = jnp.where(spot < band_rows - whole, keys[whole : whole + 8], moved)
            both = jnp.concatenate([keys[:whole], tail], axis=0)
            block_ref[...] = both[:count].astype(jnp.bfloat16)
        else:
            for i, kind in enumerate(kinds):
                cols = slice(i * own_cols, (i + 1) * own_cols)
                block_ref[:, cols] = block(kind, r)[:count].astype(jnp.bfloat16)


def select_kernel(rounds, first, picks_ref, *refs):
    outs = refs[sum(1 + rest for *_, rest in rounds) :]
    refs = iter(refs)
    band_rows = picks_ref.shape[-1]
    width = outs[0].shape[1]
    blocks = []
    for r, at, rest in rounds:
        block = next(refs)[:, at * width : (at + 1) * width]
        if rest:
            whole = block.shape[0]
            last = next(refs)[whole:, :].astype(jnp.float32)
            last = last[band_rows - whole :].astype(jnp.bfloat16)
            block = jnp.concatenate([block, last], axis=0)
        blocks.append((r, block[:band_rows]))
    for i, out in enumerate(outs):
        terms = [dot(picks_ref[first + i, r], block) for r, block in blocks]
        out[...] = sum(terms[1:], terms[0]).astype(jnp.bfloat16)


def call(kernel, out_shape, n_scalar, n_vmem, flops, moved, n_hbm=0, scratch=()):
    return pl.pallas_call(
        kernel,
        out_shape=out_shape,
        in_specs=[SMEM] * n_scalar + [VMEM] * n_vmem + [HBM] * n_hbm,
        out_specs=jax.tree.map(lambda _: VMEM, out_shape),
        scratch_shapes=list(scratch),
        compiler_params=pltpu.CompilerParams(vmem_limit_bytes=VMEM_LIMIT),
        cost_estimate=pl.CostEstimate(flops=flops, bytes_accessed=moved, transcendentals=0),
    )


def local(
    memory_in, norm_gain, qkv_weight, out_weight, key_weight, value_weight, shift_offsets, row_order
):
    _, band_rows, emb = memory_in.shape
    n_seq = lax.axis_size("seq")
    n_tensor = lax.axis_size("tensor")
    own_cols = key_weight.shape[1] // n_seq
    pos = row_order.shape[1] // n_tensor
    rows = -(-band_rows // 16) * 16
    place = jnp.stack([lax.axis_index(axis) for axis in ("seq", "tensor", "dp")]).astype(jnp.int32)
    halo = rotated(memory_in[0, GRID_W :], "seq", 1)
    order = lax.dynamic_index_in_dim(row_order, lax.axis_index("tensor"), 0, False)
    order = order.reshape(n_tensor, pos, 1)

    weights = [qkv_weight, out_weight, key_weight, value_weight]
    off_chip = [shift_offsets, memory_in, norm_gain.reshape(1, emb), *weights]
    rolled_own, take, same, picks, gain, qkv_chip, out_chip, key_chip, value_chip = call(
        stage_kernel,
        [
            jax.ShapeDtypeStruct((rows, emb), jnp.bfloat16),
            jax.ShapeDtypeStruct((rows, halo.shape[0]), jnp.bfloat16),
            jax.ShapeDtypeStruct((GRID_W // WIN, *SLAB), jnp.int32),
            jax.ShapeDtypeStruct((n_tensor, n_seq, pos, band_rows), jnp.bfloat16),
            jax.ShapeDtypeStruct((1, emb), jnp.float32),
        ]
        + [jax.ShapeDtypeStruct(w.shape, w.dtype) for w in weights],
        1, 1, 50_000_000, 8_000_000, len(off_chip),
        [
            pltpu.SMEM(shift_offsets.shape, jnp.int32),
            pltpu.VMEM((band_rows, emb), jnp.bfloat16),
            pltpu.SemaphoreType.DMA((len(off_chip),)),
        ],
    )(place, order, *(pltpu.with_memory_space_constraint(x, pltpu.HBM) for x in off_chip))

    apart = [0, *range(2, n_seq)]
    blocks = [((0,), r) for r in apart] + [((0, 1), 1)] + [((1,), r) for r in apart]
    whole = band_rows // 16 * 16
    counts = {(0,): 2 * band_rows - whole, (0, 1): band_rows, (1,): whole}
    sent = call(
        functools.partial(encode_kernel, blocks, band_rows),
        [
            jax.ShapeDtypeStruct((counts[kinds], len(kinds) * own_cols), jnp.bfloat16)
            for kinds, _ in blocks
        ],
        1, 9, 2_000_000_000, 10_000_000,
    )(place, rolled_own, halo, take, same, gain, qkv_chip, out_chip, key_chip, value_chip)
    held = [exchanged(b, r) if r else b for (_, r), b in zip(blocks, sent)]

    def selected(kind, first, count):
        mine, operands = [], []
        for (kinds, r), b in zip(blocks, held):
            if kind in kinds:
                rest = kinds == (1,)
                mine.append((r, kinds.index(kind), int(rest)))
                operands += [b, held[blocks.index(((0,), r))]] if rest else [b]
        return call(
            functools.partial(select_kernel, mine, first),
            [jax.ShapeDtypeStruct((pos, own_cols), jnp.bfloat16)] * count,
            0, 1 + len(operands), 300_000_000, 1_000_000,
        )(picks, *operands)

    def gathered(group):
        away = selected(group, 1, n_tensor - 1)
        arrived = [rotated(away[d - 1], "tensor", d) for d in range(1, n_tensor)]
        return [*selected(group, 0, 1), *arrived]

    def by_page(blocks):
        page = jnp.arange(n_tensor)[:, None, None]
        result = blocks[0][None]
        for d in range(1, n_tensor):
            came = page == (lax.axis_index("tensor") - d) % n_tensor
            result = jnp.where(came, blocks[d][None], result)
        return jnp.broadcast_to(result, (n_tensor, pos, own_cols))

    key_out, value_blocks = lax.optimization_barrier((by_page(gathered(0)), gathered(1)))
    return key_out, by_page(value_blocks)


def solution(mesh):
    placed = (
        P(("dp", "tensor"), "seq", None),
        P(),
        P(),
        P(),
        P(),
        P(),
        P(("dp", "tensor"), None),
        P("dp", None),
    )
    return jax.shard_map(
        local,
        mesh=mesh,
        in_specs=placed,
        out_specs=(P("dp", "tensor", "seq"), P("dp", "tensor", "seq")),
        check_vma=False,
    )
```

```python
import functools

import jax
import jax.numpy as jnp
from jax import lax
from jax.experimental import pallas as pl
from jax.experimental.pallas import tpu as pltpu
from jax.sharding import PartitionSpec as P

HEADS = 16
HEAD_DIM = 32
GRID_H = 28
GRID_W = 21
WIN = 7

GROUP = 4
SLAB = (56, 64)
VMEM_LIMIT = 24 * 1024 * 1024

SMEM = pl.BlockSpec(memory_space=pltpu.SMEM)
VMEM = pl.BlockSpec(memory_space=pltpu.VMEM)
HBM = pl.BlockSpec(memory_space=pltpu.HBM)


def rotated(block, axis, distance):
    devices = lax.axis_size(axis)
    return lax.ppermute(block, axis, [(i, (i + distance) % devices) for i in range(devices)])


def paired(n):
    return n & (n - 1) == 0


def rounds_of(n):
    even = [*range(1, n)]
    odd = [*even[1:2], *even[:1], *even[2:]]
    return [(0, 0), *zip(even, odd)]


def distance(place, r, n):
    even, odd = rounds_of(n)[r]
    return jnp.where(lax.rem(place[2], 2) == 0, even, odd)


def target(place, r, n):
    d = distance(place, r, n)
    return place[0] ^ d if paired(n) else lax.rem(place[0] + d, n)


def origin(place, r, n):
    d = distance(place, r, n)
    return place[0] ^ d if paired(n) else lax.rem(place[0] - d + n, n)


def exchanged(block, r):
    n = lax.axis_size("seq")
    pairs = []
    for i in range(lax.axis_size("dp")):
        d = rounds_of(n)[r][i % 2]
        pairs += [(i * n + j, i * n + (j ^ d if paired(n) else (j + d) % n)) for j in range(n)]
    return lax.ppermute(block, ("dp", "seq"), pairs)


def band_of(seq, n_seq):
    return lax.rem(seq + n_seq - 1, n_seq)


def dot(a, b):
    return jnp.dot(a, b, preferred_element_type=jnp.float32)


def one_hot(cond):
    return jnp.where(cond, 1.0, 0.0).astype(jnp.bfloat16)


def cells(index, band_rows):
    window = index // (WIN * WIN)
    inside = index - window * (WIN * WIN)
    row = inside // WIN
    return row, window * WIN + inside - row * WIN


def slab(window):
    return window * WIN * WIN // 8 * 8


def stage_kernel(place, order_ref, shifts_hbm, pages_hbm, gain_hbm, *refs):
    weights, refs = refs[:4], refs[4:]
    rolled_ref, take_ref, same_ref, picks_ref, gain_ref, *staged = refs[:9]
    shifts, own, arrived = refs[9:]
    pairs = [(shifts_hbm, shifts), (pages_hbm.at[0], own), (gain_hbm, gain_ref)]
    pairs += list(zip(weights, staged))
    copies = [pltpu.make_async_copy(*pair, arrived.at[i]) for i, pair in enumerate(pairs)]
    for copy in copies:
        copy.start()
    band_rows = own.shape[0]
    rows, halo_rows = take_ref.shape
    n_tensor, n_seq, pos, _ = picks_ref.shape
    for i in range(n_tensor):
        order = order_ref[lax.rem(place[1] + i, n_tensor)]
        order_band = order // band_rows
        row = (order - order_band * band_rows) // GRID_W
        col = order - order_band * band_rows - row * GRID_W
        window = col // WIN
        cell_at = (window * WIN + row) * WIN + col - window * WIN
        for r in range(n_seq):
            band = band_of(origin(place, r, n_seq), n_seq)
            at = jnp.where(order_band == band, cell_at, -1)
            picks_ref[i, r] = one_hot(at == lax.broadcasted_iota(jnp.int32, (1, band_rows), 1))
    copies[0].wait()
    row_shift, col_shift = shifts[0, 0], shifts[0, 1]

    cell = lax.broadcasted_iota(jnp.int32, (rows, 1), 0)
    cell_row, cell_col = cells(cell, band_rows)
    from_col = cell_col + col_shift
    from_col = jnp.where(from_col >= GRID_W, from_col - GRID_W, from_col)
    skipped = band_rows - halo_rows
    source = jnp.where(cell < band_rows, (cell_row + row_shift) * GRID_W + from_col - skipped, -1)
    take_ref[...] = one_hot(source == lax.broadcasted_iota(jnp.int32, (rows, halo_rows), 1))
    take_own = one_hot(
        source - halo_rows == lax.broadcasted_iota(jnp.int32, (rows, band_rows), 1)
    )

    band = band_of(place[0], n_seq)

    def marks(index):
        row, col = cells(index, band_rows)
        wrap_row = (band * WIN + row >= GRID_H - row_shift).astype(jnp.int32)
        wrap_col = (col >= GRID_W - col_shift).astype(jnp.int32)
        return jnp.where(index < band_rows, (col // WIN) * 4 + 2 * wrap_row + wrap_col, -1)

    windows, queries, keys = same_ref.shape
    for w in range(windows):
        query = slab(w) + lax.broadcasted_iota(jnp.int32, (queries, 1), 0)
        key = slab(w) + lax.broadcasted_iota(jnp.int32, (1, keys), 1)
        same_ref[w] = (marks(query) == marks(key)).astype(jnp.int32)
    copies[1].wait()
    rolled_ref[...] = dot(take_own, own[...]).astype(jnp.bfloat16)
    for copy in copies[2:]:
        copy.wait()


def encode_kernel(
    blocks, band_rows, place, rolled_ref, halo_ref, take_ref, same_ref, gain_ref, qkv_ref, out_ref, key_ref,
    value_ref, *sent
):
    rows = rolled_ref.shape[0]
    attn = HEADS * HEAD_DIM
    rolled = rolled_ref[...].astype(jnp.float32) + dot(take_ref[...], halo_ref[...])

    mean = jnp.mean(rolled, axis=-1, keepdims=True)
    centred = rolled - mean
    variance = jnp.mean(centred * centred, axis=-1, keepdims=True)
    normed = (centred * lax.rsqrt(variance + 1e-05) * gain_ref[...]).astype(jnp.bfloat16)
    qkv = dot(normed, qkv_ref[...])

    windows, queries, keys = same_ref.shape
    width = GROUP * HEAD_DIM
    lane_head = lax.broadcasted_iota(jnp.int32, (1, width), 1) // HEAD_DIM
    units = [(w, g) for w in range(windows) for g in range(HEADS // GROUP)]

    def taken(w, g, kind, count):
        at = kind * attn + g * width
        return qkv[slab(w) : slab(w) + count, at : at + width].astype(jnp.bfloat16)

    scores = []
    for w, g in units:
        q, k = taken(w, g, 0, queries), taken(w, g, 1, keys)
        stacked = jnp.concatenate(
            [jnp.where(lane_head == h, q, jnp.zeros_like(q)) for h in range(GROUP)], axis=0
        )
        scores.append(
            lax.dot_general(
                stacked, k, (((1,), (1,)), ((), ())), preferred_element_type=jnp.float32
            )
        )
    weights = []
    for (w, _), score in zip(units, scores):
        same = jnp.concatenate([same_ref[w]] * GROUP, axis=0) != 0
        score = jnp.where(same, score, -1000000000.0 * HEAD_DIM**0.5)
        top = jnp.max(score, axis=-1, keepdims=True)
        score = jnp.exp2((score - top) * (HEAD_DIM ** (-0.5) * 1.4426950408889634))
        total = jnp.sum(score, axis=-1, keepdims=True)
        weights.append((score.astype(jnp.bfloat16), 1.0 / total))
    parts = [[] for _ in range(HEADS // GROUP)]
    for (w, g), weight in zip(units, weights):
        mixed = dot(weight[0], taken(w, g, 2, keys)) * weight[1]
        mine = mixed[:queries]
        for h in range(1, GROUP):
            mine = jnp.where(lane_head == h, mixed[h * queries : (h + 1) * queries], mine)
        part = parts[g]
        if w == 0:
            part.append(mine)
            continue
        overlap = slab(w - 1) + queries - slab(w)
        row = slab(w) + lax.broadcasted_iota(jnp.int32, (overlap, 1), 0)
        last = part.pop()
        part.append(last[:-overlap])
        part.append(jnp.where(row < w * WIN * WIN, last[-overlap:], mine[:overlap]))
        part.append(mine[overlap:])
    pad = rows - slab(windows - 1) - queries
    parts = [
        jnp.concatenate([*part, jnp.zeros((pad, width), jnp.float32)], axis=0).astype(jnp.bfloat16)
        for part in parts
    ]
    attended = jnp.concatenate(parts, axis=1)
    memory = (rolled + dot(attended, out_ref[...])).astype(jnp.bfloat16)
    n_seq = 1 + max(r for _, r in blocks)
    own_cols = key_ref.shape[1] // n_seq

    def block(kind, r):
        at = pl.multiple_of(target(place, r, n_seq) * own_cols, own_cols)
        return dot(memory, (key_ref, value_ref)[kind][:, pl.ds(at, own_cols)])

    apart = {r for kinds, r in blocks if kinds == (0,)}
    values = {r: block(1, r) for r in apart}
    for (kinds, r), block_ref in zip(blocks, sent):
        count = block_ref.shape[0]
        if kinds == (1,):
            block_ref[...] = values[r][:count].astype(jnp.bfloat16)
        elif kinds == (0,):
            keys = block(0, r)
            whole = count // 8 * 8
            extra = count - band_rows
            spot = lax.broadcasted_iota(jnp.int32, (8, 1), 0)
            moved = pltpu.roll(values[r][whole : whole + 8], extra, 0)
            tail = jnp.where(spot < band_rows - whole, keys[whole : whole + 8], moved)
            both = jnp.concatenate([keys[:whole], tail], axis=0)
            block_ref[...] = both[:count].astype(jnp.bfloat16)
        else:
            for i, kind in enumerate(kinds):
                cols = slice(i * own_cols, (i + 1) * own_cols)
                block_ref[:, cols] = block(kind, r)[:count].astype(jnp.bfloat16)


def select_kernel(rounds, first, picks_ref, *refs):
    outs = refs[sum(1 + rest for *_, rest in rounds) :]
    refs = iter(refs)
    band_rows = picks_ref.shape[-1]
    width = outs[0].shape[1]
    blocks = []
    for r, at, rest in rounds:
        block = next(refs)[:, at * width : (at + 1) * width]
        if rest:
            whole = block.shape[0]
            last = next(refs)[whole:, :].astype(jnp.float32)
            last = last[band_rows - whole :].astype(jnp.bfloat16)
            block = jnp.concatenate([block, last], axis=0)
        blocks.append((r, block[:band_rows]))
    for i, out in enumerate(outs):
        terms = [dot(picks_ref[first + i, r], block) for r, block in blocks]
        out[...] = sum(terms[1:], terms[0]).astype(jnp.bfloat16)


def call(kernel, out_shape, n_scalar, n_vmem, flops, moved, n_hbm=0, scratch=()):
    return pl.pallas_call(
        kernel,
        out_shape=out_shape,
        in_specs=[SMEM] * n_scalar + [VMEM] * n_vmem + [HBM] * n_hbm,
        out_specs=jax.tree.map(lambda _: VMEM, out_shape),
        scratch_shapes=list(scratch),
        compiler_params=pltpu.CompilerParams(vmem_limit_bytes=VMEM_LIMIT),
        cost_estimate=pl.CostEstimate(flops=flops, bytes_accessed=moved, transcendentals=0),
    )


def local(
    memory_in, norm_gain, qkv_weight, out_weight, key_weight, value_weight, shift_offsets, row_order
):
    _, band_rows, emb = memory_in.shape
    n_seq = lax.axis_size("seq")
    n_tensor = lax.axis_size("tensor")
    own_cols = key_weight.shape[1] // n_seq
    pos = row_order.shape[1] // n_tensor
    rows = -(-band_rows // 16) * 16
    place = jnp.stack([lax.axis_index(axis) for axis in ("seq", "tensor", "dp")]).astype(jnp.int32)
    halo = rotated(memory_in[0, GRID_W :], "seq", 1)
    order = lax.dynamic_index_in_dim(row_order, lax.axis_index("tensor"), 0, False)
    order = order.reshape(n_tensor, pos, 1)

    weights = [qkv_weight, out_weight, key_weight, value_weight]
    off_chip = [shift_offsets, memory_in, norm_gain.reshape(1, emb), *weights]
    rolled_own, take, same, picks, gain, qkv_chip, out_chip, key_chip, value_chip = call(
        stage_kernel,
        [
            jax.ShapeDtypeStruct((rows, emb), jnp.bfloat16),
            jax.ShapeDtypeStruct((rows, halo.shape[0]), jnp.bfloat16),
            jax.ShapeDtypeStruct((GRID_W // WIN, *SLAB), jnp.int32),
            jax.ShapeDtypeStruct((n_tensor, n_seq, pos, band_rows), jnp.bfloat16),
            jax.ShapeDtypeStruct((1, emb), jnp.float32),
        ]
        + [jax.ShapeDtypeStruct(w.shape, w.dtype) for w in weights],
        1, 1, 50_000_000, 8_000_000, len(off_chip),
        [
            pltpu.SMEM(shift_offsets.shape, jnp.int32),
            pltpu.VMEM((band_rows, emb), jnp.bfloat16),
            pltpu.SemaphoreType.DMA((len(off_chip),)),
        ],
    )(place, order, *(pltpu.with_memory_space_constraint(x, pltpu.HBM) for x in off_chip))

    apart = [0, *range(2, n_seq)]
    blocks = [((0,), r) for r in apart] + [((0, 1), 1)] + [((1,), r) for r in apart]
    whole = band_rows // 16 * 16
    counts = {(0,): 2 * band_rows - whole, (0, 1): band_rows, (1,): whole}
    sent = call(
        functools.partial(encode_kernel, blocks, band_rows),
        [
            jax.ShapeDtypeStruct((counts[kinds], len(kinds) * own_cols), jnp.bfloat16)
            for kinds, _ in blocks
        ],
        1, 9, 2_000_000_000, 10_000_000,
    )(place, rolled_own, halo, take, same, gain, qkv_chip, out_chip, key_chip, value_chip)
    held = [exchanged(b, r) if r else b for (_, r), b in zip(blocks, sent)]

    def selected(kind, first, count):
        mine, operands = [], []
        for (kinds, r), b in zip(blocks, held):
            if kind in kinds:
                rest = kinds == (1,)
                mine.append((r, kinds.index(kind), int(rest)))
                operands += [b, held[blocks.index(((0,), r))]] if rest else [b]
        return call(
            functools.partial(select_kernel, mine, first),
            [jax.ShapeDtypeStruct((pos, own_cols), jnp.bfloat16)] * count,
            0, 1 + len(operands), 300_000_000, 1_000_000,
        )(picks, *operands)

    def gathered(group):
        away = selected(group, 1, n_tensor - 1)
        arrived = [rotated(away[d - 1], "tensor", d) for d in range(1, n_tensor)]
        return [*selected(group, 0, 1), *arrived]

    def by_page(blocks):
        page = jnp.arange(n_tensor)[:, None, None]
        result = blocks[0][None]
        for d in range(1, n_tensor):
            came = page == (lax.axis_index("tensor") - d) % n_tensor
            result = jnp.where(came, blocks[d][None], result)
        return jnp.broadcast_to(result, (n_tensor, pos, own_cols))

    key_out, value_blocks = lax.optimization_barrier((by_page(gathered(0)), gathered(1)))
    return key_out, by_page(value_blocks)


def solution(mesh):
    placed = (
        P(("dp", "tensor"), "seq", None),
        P(),
        P(),
        P(),
        P(),
        P(),
        P(("dp", "tensor"), None),
        P("dp", None),
    )
    return jax.shard_map(
        local,
        mesh=mesh,
        in_specs=placed,
        out_specs=(P("dp", "tensor", "seq"), P("dp", "tensor", "seq")),
        check_vma=False,
    )
```
